32 devices in a mesh: dp: 4 (over z), fsdp: 8 (over y, x, core).
Axes of the slice: x: 2, y: 2, z: 4, core: 2. Of those that a mesh axis runs over, the one named last changes fastest.
Arguments:
- x_in: bfloat16 [32768, 512], P(('dp', 'fsdp')), may hold values from -6 to 6
- y_in: float32 [32768, 512], P(('dp', 'fsdp')), may hold values from -6 to 6
- lengths: int32 [32, 16], P(('dp', 'fsdp')), may hold values from 0 to 1024, as said below
- w_qkv: bfloat16 [512, 1536], P(('dp', 'fsdp')), may hold values from -0.25 to 0.25
- w_out: bfloat16 [512, 512], P(('dp', 'fsdp')), may hold values from -1 to 1
- gain_one: bfloat16 [512], P(('dp', 'fsdp')), may hold values from 0.5 to 1.5
- bias_one: bfloat16 [512], P(('dp', 'fsdp')), may hold values from -0.5 to 0.5
- w_up: bfloat16 [512, 2048], P(('dp', 'fsdp')), may hold values from -0.25 to 0.25
- b_up: bfloat16 [2048], P(('dp', 'fsdp')), may hold values from -0.5 to 0.5
- w_down: bfloat16 [2048, 512], P(('dp', 'fsdp')), may hold values from -0.125 to 0.125
- gain_two: bfloat16 [512], P(('dp', 'fsdp')), may hold values from 0.5 to 1.5
- bias_two: bfloat16 [512], P(('dp', 'fsdp')), may hold values from -0.5 to 0.5
- grad_x: bfloat16 [32768, 512], P(('dp', 'fsdp')), may hold values from -6 to 6
- grad_y: bfloat16 [32768, 512], P(('dp', 'fsdp')), may hold values from -6 to 6
Outputs:
- x_out: bfloat16 [32768, 512], P(('dp', 'fsdp'))
- y_out: float32 [32768, 512], P(('dp', 'fsdp'))
- d_x: float32 [32768, 512], P(('dp', 'fsdp'))
- d_qkv: float32 [512, 1536], P(('dp', 'fsdp'))
- d_out: float32 [512, 512], P(('dp', 'fsdp'))
- d_gain_one: float32 [512], P(('dp', 'fsdp'))
- d_bias_one: float32 [512], P(('dp', 'fsdp'))
- d_up: float32 [512, 2048], P(('dp', 'fsdp'))
- d_b_up: float32 [2048], P(('dp', 'fsdp'))
- d_down: float32 [2048, 512], P(('dp', 'fsdp'))
- d_gain_two: float32 [512], P(('dp', 'fsdp'))
- d_bias_two: float32 [512], P(('dp', 'fsdp'))
The draws below stay inside these ranges and needn't reach their ends.
Inputs may be any that keep to these rules, and one draw needn't show every extreme that they name: `lengths`: row g lists the sequences of slot group g in slot order; the first entry is positive, zeros are unused entries, each row sums to at most 1024, and in every draw some row holds a single sequence of exactly 1024 tokens.
All inputs are finite; a program needn't handle non-finite values.
Results may differ from the reference program's by a relative error of at most 0.012.
Values may be sent and summed in bfloat16 or wider, within the bound.
A program may use at most 192 MiB of HBM per device.

```python
import jax
import jax.numpy as jnp
from jax import lax

D = 512
H = 8
HD = 64
FF = 2048
CAP = 1024
SEQS = 16
SHORT = 128
TOKENS = 32768
N_DP = 4
N_FSDP = 8


def draw_lengths(key, part):
    key = jax.random.fold_in(key, 11)
    keys = jax.random.split(key, 5)
    groups = N_DP * N_FSDP
    counted = jax.random.randint(keys[0], (groups, 1), 1, SEQS + 1)
    drawn = jax.random.randint(keys[1], (groups, SEQS), 4, SHORT + 1)
    with_long = jax.random.randint(keys[2], (groups,), 0, 4) == 0
    long_length = jax.random.randint(keys[3], (groups,), CAP // 4, CAP + 1)
    column = jnp.arange(SEQS)[None, :]
    drawn = jnp.where((column == 0) & with_long[:, None], long_length[:, None], drawn)
    drawn = jnp.where(column < counted, drawn, 0)
    before = jnp.cumsum(drawn, axis=1) - drawn
    capped = jnp.minimum(drawn, jnp.maximum(CAP - before, 0))
    chosen = jax.random.randint(keys[4], (), 0, groups)
    full_row = jnp.where(column == 0, CAP, 0)
    capped = jnp.where(jnp.arange(groups)[:, None] == chosen, full_row, capped)
    return capped.astype(jnp.int32)


def shard_levels(stream_key, shape, shards, smallest, top_value):
    loudness, own = 1.0, jax.random.fold_in(stream_key, 6)
    for dim, shards_of in shards:
        steps = jnp.exp(jax.random.uniform(jax.random.fold_in(own, dim), (shards_of,), jnp.float32, smallest / len(shards), top_value / len(shards)))
        loudness = loudness * jnp.repeat(steps, shape[dim] // shards_of).reshape([-1 if axis == dim else 1 for axis in range(len(shape))])
    return loudness


def noise(own_key, dims, width, most, shards=(), held_as=jnp.bfloat16):
    factor_of = shard_levels(own_key, dims, shards, -0.22, 0.18) if shards else 1.0
    entries = jax.random.normal(own_key, dims, jnp.float32) * width * factor_of
    return jnp.minimum(jnp.maximum(entries, -most), most).astype(held_as)


def setup_inputs(seed: int = 0) -> dict:
    splits = jax.random.split(jax.random.key(seed), 15)
    return {
        "x_in": noise(splits[0], (TOKENS, D), 1.0, 6.0, ((0, 32),)),
        "y_in": noise(splits[1], (TOKENS, D), 1.0, 6.0, ((0, 32),), jnp.float32),
        "lengths": draw_lengths(jax.random.fold_in(splits[14], 71), 0),
        "w_qkv": noise(splits[3], (D, 3 * D), D ** -0.5, 0.25, ((0, 32),)),
        "w_out": noise(splits[4], (D, D), (D // 16) ** -0.5, 1.0, ((0, 32),)),
        "gain_one": jnp.clip(1.0 + 0.1 * jax.random.normal(splits[5], (D,), jnp.float32), 0.5, 1.5).astype(jnp.bfloat16),
        "bias_one": jnp.clip(jax.random.uniform(splits[6], (D,), jnp.float32, -0.5, 0.5) * shard_levels(splits[6], (D,), ((0, 32),), -0.4, 0.0), -0.5, 0.5).astype(jnp.bfloat16),
        "w_up": noise(splits[7], (D, FF), D ** -0.5, 0.25, ((0, 32),)),
        "b_up": jnp.clip(jax.random.uniform(splits[8], (FF,), jnp.float32, -0.5, 0.5) * shard_levels(splits[8], (FF,), ((0, 32),), -0.4, 0.0), -0.5, 0.5).astype(jnp.bfloat16),
        "w_down": noise(splits[9], (FF, D), FF ** -0.5, 0.125, ((0, 32),)),
        "gain_two": jnp.clip(1.0 + 0.1 * jax.random.normal(splits[10], (D,), jnp.float32), 0.5, 1.5).astype(jnp.bfloat16),
        "bias_two": jnp.clip(jax.random.uniform(splits[11], (D,), jnp.float32, -0.5, 0.5) * shard_levels(splits[11], (D,), ((0, 32),), -0.4, 0.0), -0.5, 0.5).astype(jnp.bfloat16),
        "grad_x": noise(splits[12], (TOKENS, D), 1.0, 6.0, ((0, 32),)),
        "grad_y": noise(splits[13], (TOKENS, D), 1.0, 6.0, ((0, 32),)),
    }


@jax.custom_vjp
def low(v):
    return lax.optimization_barrier(v.astype(jnp.bfloat16)).astype(jnp.float32)

@jax.custom_vjp
def low_back(v):
    return v

def low_keep(v):
    return (low(v), None)

def low_pass(kept, grad):
    return (grad,)

def back_keep(v):
    return (v, None)

def back_low(kept, grad):
    return (low(grad),)
low.defvjp(low_keep, low_pass)
low_back.defvjp(back_keep, back_low)
EPSILON = 1e-05
NEGATIVE = -1e+30
HIGH = lax.Precision.HIGHEST

def layer_norm(summed, gain_vec, bias_vec):
    average = lax.optimization_barrier(jnp.mean(summed, axis=-1, keepdims=True))
    centred = summed - average
    spread = lax.optimization_barrier(jnp.mean(centred * centred, axis=-1, keepdims=True))
    return centred * lax.rsqrt(spread + EPSILON) * gain_vec + bias_vec

def slot_layout(lengths_row):
    bounds = jnp.cumsum(lengths_row)
    position = jnp.arange(CAP, dtype=jnp.int32)
    segment = lax.optimization_barrier(jnp.sum((bounds[None, :] <= position[:, None]).astype(jnp.int32), axis=1))
    active = position < bounds[-1]
    segment = jnp.where(active, segment, -1 - position)
    return (position, segment, active.astype(jnp.float32)[:, None])

def group_forward(weights, inputs):
    w_qkv, w_out, gain_one, bias_one, w_up, b_up, w_down, gain_two, bias_two = weights
    x_rows, y_rows, lengths_row = inputs
    position, segment, active = slot_layout(lengths_row)
    qkv = low(low_back(jnp.dot(x_rows, w_qkv, precision=HIGH)))
    queries = qkv[:, :D].reshape(CAP, H, HD)
    keys_all = qkv[:, D:2 * D].reshape(CAP, H, HD)
    values_all = qkv[:, 2 * D:].reshape(CAP, H, HD)
    factor = HD ** (-0.5)
    raw = jnp.einsum('qhd,khd->hqk', queries, keys_all, precision=HIGH) * factor
    raw = low_back(raw)
    allowed = (segment[:, None] == segment[None, :]) & (position[None, :] <= position[:, None])
    scores = jnp.where(allowed[None], raw, NEGATIVE)
    row_max = lax.optimization_barrier(jnp.max(scores, axis=-1, keepdims=True))
    expd = jnp.exp(scores - row_max)
    probs = low(expd / lax.optimization_barrier(jnp.sum(expd, axis=-1, keepdims=True)))
    attended = jnp.einsum('hqk,khd->qhd', probs, values_all, precision=HIGH).reshape(CAP, D)
    attended = low(low_back(attended))
    branch_a = low_back(jnp.dot(attended, w_out, precision=HIGH))
    x_mid = layer_norm(x_rows + branch_a, gain_one, bias_one)
    y_mid = y_rows + branch_a
    upper = low_back(jnp.dot(low(x_mid), w_up, precision=HIGH) + b_up)
    hidden = low(jax.nn.gelu(upper, approximate=True))
    branch_f = low_back(jnp.dot(hidden, w_down, precision=HIGH))
    x_next = layer_norm(x_mid + branch_f, gain_two, bias_two)
    y_next = y_mid + branch_f
    return (x_next * active, y_next * active)

def forward(x_all, y_all, lengths, weights):
    groups = lengths.shape[0]
    step = jax.checkpoint(lambda inputs: group_forward(weights, inputs))
    x_next, y_next = lax.map(step, (x_all.reshape(groups, CAP, D), y_all.reshape(groups, CAP, D), lengths))
    return (x_next.reshape(-1, D), y_next.reshape(-1, D))

def reference(x_in, y_in, lengths, w_qkv, w_out, gain_one, bias_one, w_up, b_up, w_down, gain_two, bias_two, grad_x, grad_y):
    x_full = x_in.astype(jnp.float32)
    y_full = y_in.astype(jnp.float32)
    weights = tuple((w.astype(jnp.float32) for w in (w_qkv, w_out, gain_one, bias_one, w_up, b_up, w_down, gain_two, bias_two)))

    def wrapped(x_value, *weight_values):
        return forward(x_value, y_full, lengths, weight_values)
    outputs, backward = jax.vjp(wrapped, x_full, *weights)
    grads = backward((grad_x.astype(jnp.float32), grad_y.astype(jnp.float32)))
    return (outputs[0].astype(jnp.bfloat16), outputs[1], grads[0], grads[1], grads[2], grads[3], grads[4], grads[5], grads[6], grads[7], grads[8], grads[9])
```

```python
import functools

import jax
import jax.numpy as jnp
from jax import lax
from jax.experimental import pallas as pl
from jax.experimental.pallas import tpu as pltpu
from jax.sharding import PartitionSpec as P

H = 8
PAIR = 128
HALF = 64
BLOCK = 256
CHUNK = 512
GRID = (4, 2, 2, 2)
ROWS = 16
Z = GRID[0]
PIECES = 12
VMEM_LIMIT = 67000000
EPSILON = 1e-05
NEGATIVE = -1e30
GELU_C = 0.7978845608028654
GELU_K = 0.044715
F32 = jnp.float32
BF16 = jnp.bfloat16
MESH = pl.DeviceIdType.MESH


def mm(a, b):
    return lax.dot_general(a, b, (((1,), (0,)), ((), ())), preferred_element_type=F32)


def mm_nt(a, b):
    return lax.dot_general(a, b, (((1,), (1,)), ((), ())), preferred_element_type=F32)


def mm_tn(a, b):
    return lax.dot_general(a, b, (((0,), (0,)), ((), ())), preferred_element_type=F32)


class Place:
    def __init__(self):
        self.z = lax.axis_index("dp")
        inner = lax.axis_index("fsdp")
        self.c = lax.rem(inner, 2)
        self.x = lax.rem(inner // 2, 2)
        self.y = inner // 4

    def device(self, z, y, x, c):
        return (z, (y * 2 + x) * 2 + c)

    def first(self, p):
        odd = p % 2
        return (self.y + odd) % 2, (self.x + 1 - odd) % 2

    def second(self, p):
        odd = p % 2
        return (self.y + 1 - odd) % 2, (self.x + odd) % 2

    def around(self, d):
        return lax.rem(self.z + d, Z)


class Gather:
    def __init__(self, place, buf, send, recv):
        self.at, self.buf, self.send, self.recv = place, buf, send, recv

    def copy(self, block, target, p, n):
        ref = self.buf.at[block]
        return pltpu.make_async_remote_copy(
            src_ref=ref,
            dst_ref=ref,
            send_sem=self.send.at[p, n],
            recv_sem=self.recv.at[p, n],
            device_id=target,
            device_id_type=MESH,
        )

    def along_z(self, p, d, source):
        a = self.at
        return self.copy((p, source, a.y, a.x, a.c), a.device(a.around(d), a.y, a.x, a.c), p, d - 1)

    def plane(self, p, n, y, x, to):
        a = self.at
        return self.copy((p, slice(None), y, x, a.c), a.device(a.z, to[0], to[1], a.c), p, n)

    def core(self, p, c):
        a = self.at
        every = slice(None)
        return self.copy((p, every, every, every, c), a.device(a.z, a.y, a.x, 1 - a.c), p, Z + 2)

    def step(self, n, p):
        a = self.at
        y1, x1 = a.first(p)
        y2, x2 = a.second(p)
        if n == 0:
            for d in range(1, Z):
                self.along_z(p, d, a.z).start()
        elif n == 1:
            for d in range(1, Z):
                self.along_z(p, d, a.around(Z - d)).wait_recv()
            self.plane(p, Z - 1, a.y, a.x, (y1, x1)).start()
            self.plane(p, Z, a.y, a.x, (y2, x2)).start()
        elif n == 2:
            self.plane(p, Z - 1, y1, x1, (y1, x1)).wait_recv()
            self.plane(p, Z + 1, y1, x1, (y2, x2)).start()
        elif n == 3:
            self.plane(p, Z, y2, x2, (y2, x2)).wait_recv()
            self.plane(p, Z + 1, 1 - a.y, 1 - a.x, (y2, x2)).wait_recv()
            self.core(p, a.c).start()
        elif n == 4:
            self.core(p, 1 - a.c).wait_recv()
        else:
            for d in range(1, Z):
                self.along_z(p, d, a.z).wait_send()
            self.plane(p, Z - 1, a.y, a.x, (y1, x1)).wait_send()
            self.plane(p, Z, a.y, a.x, (y2, x2)).wait_send()
            self.plane(p, Z + 1, y1, x1, (y2, x2)).wait_send()
            self.core(p, a.c).wait_send()


class Scatter:
    def __init__(self, place, buf, got_core, got_first, got_second, got_z, send, recv, finish):
        self.at, self.buf = place, buf
        self.got_core, self.got_first = got_core, got_first
        self.got_second, self.got_z = got_second, got_z
        self.send, self.recv, self.finish = send, recv, finish

    def copy(self, src, dst, target, p, n):
        return pltpu.make_async_remote_copy(
            src_ref=src,
            dst_ref=dst,
            send_sem=self.send.at[p, n],
            recv_sem=self.recv.at[p, n],
            device_id=target,
            device_id_type=MESH,
        )

    def core(self, p):
        a = self.at
        every = slice(None)
        return self.copy(
            self.buf.at[p, every, every, every, 1 - a.c],
            self.got_core.at[p],
            a.device(a.z, a.y, a.x, 1 - a.c),
            p,
            0,
        )

    def plane(self, p, n, y, x, to):
        a = self.at
        dst = self.got_second.at[p] if n == 3 else self.got_first.at[p, n - 1]
        target = a.device(a.z, to[0], to[1], a.c)
        return self.copy(self.buf.at[p, :, y, x, a.c], dst, target, p, n)

    def along_z(self, p, d):
        a = self.at
        z = a.around(d)
        return self.copy(
            self.buf.at[p, z, a.y, a.x, a.c],
            self.got_z.at[p, d - 1],
            a.device(z, a.y, a.x, a.c),
            p,
            3 + d,
        )

    def add(self, block, value):
        self.buf[block] = (self.buf[block].astype(F32) + value.astype(F32)).astype(BF16)

    def step(self, n, p):
        a = self.at
        y1, x1 = a.first(p)
        y2, x2 = a.second(p)
        every = slice(None)
        if n == 0:
            self.core(p).start()
        elif n == 1:
            self.core(p).wait_recv()
            self.add((p, every, every, every, a.c), self.got_core[p])
            self.plane(p, 1, 1 - a.y, 1 - a.x, (y1, x1)).start()
            self.plane(p, 2, y1, x1, (y1, x1)).start()
        elif n == 2:
            self.plane(p, 1, 1 - a.y, 1 - a.x, (y1, x1)).wait_recv()
            self.add((p, every, y2, x2, a.c), self.got_first[p, 0])
            self.plane(p, 3, y2, x2, (y2, x2)).start()
            self.plane(p, 2, y1, x1, (y1, x1)).wait_recv()
            self.add((p, every, a.y, a.x, a.c), self.got_first[p, 1])
        elif n == 3:
            self.plane(p, 3, y2, x2, (y2, x2)).wait_recv()
            self.add((p, every, a.y, a.x, a.c), self.got_second[p])
            for d in range(1, Z):
                self.along_z(p, d).start()
        elif n == 4:
            total = self.buf[p, a.z, a.y, a.x, a.c].astype(F32)
            for d in range(1, Z):
                self.along_z(p, d).wait_recv()
                total = total + self.got_z[p, d - 1].astype(F32)
            self.finish(p, total)
        else:
            self.core(p).wait_send()
            self.plane(p, 1, 1 - a.y, 1 - a.x, (y1, x1)).wait_send()
            self.plane(p, 2, y1, x1, (y1, x1)).wait_send()
            self.plane(p, 3, y2, x2, (y2, x2)).wait_send()
            for d in range(1, Z):
                self.along_z(p, d).wait_send()


def as_matrix(value):
    return value.reshape(-1, value.shape[-1])


def layer_kernel(linked, *refs):
    refs = list(refs)

    def take(n):
        out = refs[:n]
        del refs[:n]
        return out

    lengths_ref, x_hbm, y_hbm, gx_hbm, gy_hbm = take(5)
    if linked:
        s_qkv, s_out, s_up, s_down, s_small = take(5)
        xo_hbm, yo_hbm, dx_hbm, o_qkv, o_out, o_up, o_down, o_small = take(8)
        weights, grads, small, g_small = take(4)
        got = take(8)
        sems = take(8)
    else:
        weights, small = take(2)
        xo_hbm, yo_hbm, dx_hbm, grads, g_small = take(5)
    (
        x_ref,
        y_buf,
        gx_buf,
        gy_buf,
        dx_ref,
        params,
        sums,
        qkv_ref,
        att_t,
        datt,
        datt_t,
        probs,
        bias,
        hidden,
        du_ref,
        x_low,
        df_ref,
        x_t,
        s_scr,
        in_sem,
        out_sem,
    ) = refs

    slots, width = x_ref.shape
    nblk = slots // BLOCK
    ff = hidden.shape[1]
    pairs = H // 2
    per = ff // CHUNK

    loads = []
    for n, (src, dst) in enumerate(
        ((x_hbm, x_ref), (y_hbm, y_buf), (gx_hbm, gx_buf), (gy_hbm, gy_buf))
    ):
        cp = pltpu.make_async_copy(src, dst, in_sem.at[n])
        cp.start()
        loads.append(cp)

    if linked:
        place = Place()
        z, y, x, c = place.z, place.y, place.x, place.c
        barrier = pltpu.get_barrier_semaphore()
        partners = [
            place.device(z, y, x, 1 - c),
            place.device(z, y, 1 - x, c),
            place.device(z, 1 - y, x, c),
        ] + [place.device(place.around(d), y, x, c) for d in range(1, Z)]
        for partner in partners:
            pl.semaphore_signal(barrier, inc=1, device_id=partner, device_id_type=MESH)
        for g in range(pairs):
            lanes = [slice(n * width + g * PAIR, n * width + (g + 1) * PAIR) for n in range(3)]
            own = [s_qkv[:, lane] for lane in lanes] + [s_out[:, lanes[0]]]
            weights[g, z, y, x, c] = jnp.concatenate(own, axis=1)
        for j in range(per):
            weights[pairs + j, z, y, x, c] = s_up[:, j * CHUNK : (j + 1) * CHUNK]
            weights[pairs + per + j, z, y, x, c] = s_down[j * ROWS : (j + 1) * ROWS, :]
        small[0, z, y, x, c] = s_small[...]
        pl.semaphore_wait(barrier, len(partners))

        def finish(p, total):
            if isinstance(p, int):
                if p < pairs:
                    for n in range(3):
                        lane = slice(n * width + p * PAIR, n * width + (p + 1) * PAIR)
                        o_qkv[:, lane] = total[:, n * PAIR : (n + 1) * PAIR]
                    o_out[:, p * PAIR : (p + 1) * PAIR] = total[:, 3 * PAIR :]
                elif p < pairs + per:
                    o_up[:, (p - pairs) * CHUNK : (p - pairs + 1) * CHUNK] = total
                else:
                    at = (p - pairs - per) * ROWS
                    o_down[at : at + ROWS, :] = total

        def finish_small(p, total):
            o_small[...] = total

        gather = Gather(place, weights, sems[0], sems[1])
        gather_small = Gather(place, small, sems[2], sems[3])
        scatter = Scatter(place, grads, *got[:4], sems[4], sems[5], finish)
        scatter_small = Scatter(place, g_small, *got[4:], sems[6], sems[7], finish_small)
        for n in range(5):
            gather_small.step(n, 0)
            for p in range(PIECES):
                gather.step(n, p)

    def segments(pos):
        seg = jnp.zeros(pos.shape, jnp.int32)
        end = jnp.int32(0)
        for j in range(lengths_ref.shape[1]):
            end = end + lengths_ref[0, j]
            seg = seg + (end <= pos).astype(jnp.int32)
        return jnp.where(pos < end, seg, -1 - pos), end

    starts = [BLOCK * (qb * (qb + 1) // 2) for qb in range(nblk)]
    for qb in range(nblk):
        q_pos = lax.broadcasted_iota(jnp.int32, (1, BLOCK), 1) + qb * BLOCK
        q_seg, total = segments(q_pos)
        for kb in range(qb + 1):
            k_pos = lax.broadcasted_iota(jnp.int32, (BLOCK, 1), 0) + kb * BLOCK
            k_seg, _ = segments(k_pos)
            allowed = k_seg == q_seg
            if kb == qb:
                allowed = allowed & (k_pos <= q_pos)
            at = starts[qb] + kb * BLOCK
            bias[at : at + BLOCK, :] = jnp.where(allowed, 0.0, NEGATIVE).astype(F32)

    loads[0].wait()
    x_t[...] = x_ref[...].T

    def spread(first, at, r):
        rows = first.shape[0]
        column = lax.broadcasted_iota(jnp.int32, (PAIR, width), 1)
        pick = (lax.broadcasted_iota(jnp.int32, (PAIR, width), 0) == at + column % r).astype(BF16)
        own = lax.broadcasted_iota(jnp.int32, (rows, width), 0)
        mine = own == (lax.broadcasted_iota(jnp.int32, (rows, width), 1) // r) * ROWS
        return jnp.sum(jnp.where(mine, mm(first, pick), 0.0), axis=0, keepdims=True)

    blocks = as_matrix(small[0])
    for n in range(4):
        params[n : n + 1, :width] = spread(blocks, n * ROWS, ROWS)
    for j in range(per):
        rows = blocks.shape[0] // per
        params[4:5, j * CHUNK : (j + 1) * CHUNK] = spread(
            blocks[j * rows : (j + 1) * rows], 4 * ROWS, ff * ROWS // width
        )

    lane = lax.broadcasted_iota(jnp.int32, (BLOCK, PAIR), 1)
    sub = lax.broadcasted_iota(jnp.int32, (PAIR, BLOCK), 0)

    def one_head(index, value, a):
        keep = index < HALF if a == 0 else index >= HALF
        return jnp.where(keep, value.astype(F32), 0.0).astype(BF16)

    def w_qkv(g):
        return as_matrix(weights[g, ..., : 3 * PAIR])

    def w_out():
        return jnp.concatenate(
            [as_matrix(weights[g, ..., 3 * PAIR :]) for g in range(pairs)], axis=1
        )

    def w_up(j):
        return as_matrix(weights[pairs + j])

    def w_down(j):
        parts = [weights[pairs + per + n, j].reshape(-1, ROWS, width) for n in range(per)]
        return as_matrix(jnp.stack(parts, axis=1))

    def attend(g, carry):
        for qb in range(nblk):
            rows = slice(qb * BLOCK, (qb + 1) * BLOCK)
            part = mm(x_ref[rows, :], w_qkv(g))
            q = part[:, :PAIR].astype(BF16).astype(F32) * (HALF**-0.5)
            qkv_ref[g, rows, :] = jnp.concatenate([q, part[:, PAIR:]], axis=1).astype(BF16)
        v_t = qkv_ref[g, :, 2 * PAIR :].T
        for qb in range(nblk):
            for a in range(2):
                rows = slice(qb * BLOCK, (qb + 1) * BLOCK)
                q = one_head(lane, qkv_ref[g, rows, :PAIR], a)
                top = None
                for kb in range(qb + 1):
                    k = qkv_ref[g, kb * BLOCK : (kb + 1) * BLOCK, PAIR : 2 * PAIR]
                    at = starts[qb] + kb * BLOCK
                    s = mm_nt(k, q) + bias[at : at + BLOCK, :]
                    s_scr[a, kb] = s
                    high = jnp.max(s, axis=0, keepdims=True)
                    top = high if top is None else jnp.maximum(top, high)
                whole = None
                for kb in range(qb + 1):
                    e = jnp.exp(s_scr[a, kb] - top)
                    s_scr[a, kb] = e
                    one = jnp.sum(e, axis=0, keepdims=True)
                    whole = one if whole is None else whole + one
                inverse = 1.0 / whole
                out = None
                for kb in range(qb + 1):
                    at = starts[qb] + kb * BLOCK
                    p = (s_scr[a, kb] * inverse).astype(BF16)
                    probs[2 * g + a, at : at + BLOCK, :] = p
                    o = mm(v_t[a * HALF : (a + 1) * HALF, kb * BLOCK : (kb + 1) * BLOCK], p)
                    out = o if out is None else out + o
                att_t[g, a * HALF : (a + 1) * HALF, rows] = out.astype(BF16)
        return carry

    lax.fori_loop(0, pairs, attend, 0)

    for cp in loads[1:]:
        cp.wait()

    sums[...] = jnp.zeros_like(sums)
    gain_one = params[0:1, :width]
    bias_one = params[1:2, :width]
    gain_two = params[2:3, :width]
    bias_two = params[3:4, :width]

    def norm(value):
        mean = jnp.mean(value, axis=1, keepdims=True)
        centred = value - mean
        var = jnp.mean(centred * centred, axis=1, keepdims=True)
        inv = lax.rsqrt(var + EPSILON)
        return centred * inv, inv

    def norm_back(grad, gain, n, inv):
        gn = grad * gain
        m1 = jnp.mean(gn, axis=1, keepdims=True)
        m2 = jnp.mean(gn * n, axis=1, keepdims=True)
        return (gn - m1 - n * m2) * inv

    def add_sum(row, at, value):
        sums[row : row + 1, at : at + value.shape[1]] += jnp.sum(value, axis=0, keepdims=True)

    def out_copies(rows, i):
        return (
            pltpu.make_async_copy(gx_buf.at[rows, :], xo_hbm.at[rows, :], out_sem.at[0, i]),
            pltpu.make_async_copy(y_buf.at[rows, :], yo_hbm.at[rows, :], out_sem.at[1, i]),
        )

    def slab(j, n):
        return divmod(j * (CHUNK // BLOCK) + n, nblk)

    def rows_of_tile(i, carry):
        r0 = pl.multiple_of(i * BLOCK, BLOCK)
        rows = pl.ds(r0, BLOCK)
        at_tile = att_t[:, :, rows].reshape(width, BLOCK).T
        branch_a = mm(at_tile, w_out())
        n1, inv1 = norm(x_ref[rows, :].astype(F32) + branch_a)
        x_mid = n1 * gain_one + bias_one
        xl = x_mid.astype(BF16)
        x_low[rows, :] = xl
        branch_f = None
        for j in range(per):
            cols = slice(j * CHUNK, (j + 1) * CHUNK)
            u = mm(xl, w_up(j)) + params[4:5, cols]
            u2 = u * u
            t = jnp.tanh(u * (GELU_C + (GELU_C * GELU_K) * u2))
            h = 0.5 + 0.5 * t
            low = (u * h).astype(BF16)
            hidden[rows, cols] = low
            slope = h + h * (1.0 - h) * (u * (2.0 * GELU_C + (6.0 * GELU_C * GELU_K) * u2))
            for n in range(CHUNK // BLOCK):
                s_scr[slab(j, n)] = slope[:, n * BLOCK : (n + 1) * BLOCK]
            part = mm(low, w_down(j))
            branch_f = part if branch_f is None else branch_f + part
        n2, inv2 = norm(x_mid + branch_f)
        live = (lax.broadcasted_iota(jnp.int32, (BLOCK, width), 0) + r0) < total
        gx = jnp.where(live, gx_buf[rows, :].astype(F32), 0.0)
        gy = jnp.where(live, gy_buf[rows, :].astype(F32), 0.0)
        gx_buf[rows, :] = jnp.where(live, n2 * gain_two + bias_two, 0.0).astype(BF16)
        y_buf[rows, :] = jnp.where(live, y_buf[rows, :] + branch_a + branch_f, 0.0)
        for cp in out_copies(rows, i):
            cp.start()
        add_sum(3, 0, gx)
        add_sum(2, 0, gx * n2)
        dr2 = norm_back(gx, gain_two, n2, inv2)
        df = (dr2 + gy).astype(BF16)
        df_ref[rows, :] = df
        dx_mid = dr2
        for j in range(per):
            cols = slice(j * CHUNK, (j + 1) * CHUNK)
            slope = jnp.concatenate([s_scr[slab(j, n)] for n in range(CHUNK // BLOCK)], axis=1)
            du = (mm_nt(df, w_down(j)) * slope).astype(BF16)
            du_ref[rows, cols] = du
            add_sum(4, j * CHUNK, du.astype(F32))
            dx_mid = dx_mid + mm_nt(du, w_up(j))
        add_sum(1, 0, dx_mid)
        add_sum(0, 0, dx_mid * n1)
        dr1 = norm_back(dx_mid, gain_one, n1, inv1)
        dx_ref[rows, :] = dr1
        da = (dr1 + gy).astype(BF16)
        gy_buf[rows, :] = da
        datt[rows, :] = mm_nt(da, w_out()).astype(BF16)
        datt_t[:, :, rows] = mm_nt(w_out(), da).astype(BF16).reshape(pairs, PAIR, BLOCK)
        return carry

    lax.fori_loop(0, nblk, rows_of_tile, 0)

    def put(p, at, value):
        grads[p, ..., at : at + value.shape[1]] = value.astype(BF16).reshape(
            GRID + (ROWS, value.shape[1])
        )

    for j in range(per):
        part = mm_tn(hidden[:, j * CHUNK : (j + 1) * CHUNK], df_ref[...]).astype(BF16)
        part = part.reshape(-1, per, ROWS, width)
        for n in range(per):
            grads[pairs + per + n, j] = part[:, n].reshape(GRID[1:] + (ROWS, width))
    for j in range(per):
        put(pairs + j, 0, mm_tn(x_low[...], du_ref[:, j * CHUNK : (j + 1) * CHUNK]))
    part = mm(att_t[...].reshape(width, slots), gy_buf[...])
    for g in range(pairs):
        put(g, 3 * PAIR, part[:, g * PAIR : (g + 1) * PAIR])

    def gathered(row, at, r):
        value = jnp.broadcast_to(row, (row.shape[1] * ROWS // r, width))
        own = lax.broadcasted_iota(jnp.int32, value.shape, 0) // ROWS
        mine = own == lax.broadcasted_iota(jnp.int32, value.shape, 1) // r
        column = lax.broadcasted_iota(jnp.int32, (width, PAIR), 0)
        pick = (lax.broadcasted_iota(jnp.int32, (width, PAIR), 1) == at + column % r).astype(BF16)
        return mm(jnp.where(mine, value, 0.0).astype(BF16), pick)

    rest = [
        gathered(sums[4:5, j * CHUNK : (j + 1) * CHUNK], 4 * ROWS, ff * ROWS // width)
        for j in range(per)
    ]
    rest = jnp.concatenate(rest, axis=0)
    for n in range(4):
        rest = rest + gathered(sums[n : n + 1, :width], n * ROWS, ROWS)
    g_small[0] = rest.astype(BF16).reshape(GRID + (ROWS, PAIR))

    def attend_back(g, carry):
        k_t = qkv_ref[g, :, PAIR : 2 * PAIR].T
        s_scr[0] = jnp.zeros((nblk, BLOCK, BLOCK), F32)
        lanes = pl.ds(pl.multiple_of(g * PAIR, PAIR), PAIR)
        dq_blocks = []
        for qb in range(nblk):
            rows = slice(qb * BLOCK, (qb + 1) * BLOCK)
            dq_parts = []
            for a in range(2):
                heads = slice(a * HALF, (a + 1) * HALF)
                q = one_head(lane, qkv_ref[g, rows, :PAIR], a)
                do = one_head(lane, datt[rows, lanes], a)
                do_t = one_head(sub, datt_t[g, :, rows], a)
                dots = jnp.sum(
                    att_t[g, heads, rows].astype(F32) * datt_t[g, heads, rows].astype(F32),
                    axis=0,
                    keepdims=True,
                )
                dq = None
                for kb in range(qb + 1):
                    keys = slice(kb * BLOCK, (kb + 1) * BLOCK)
                    at = starts[qb] + kb * BLOCK
                    p = probs[2 * g + a, at : at + BLOCK, :]
                    s_scr[0, kb, :, PAIR:] += mm(p, do)
                    dp = mm(qkv_ref[g, keys, 2 * PAIR :], do_t)
                    ds = (p.astype(F32) * (dp - dots)).astype(BF16)
                    s_scr[0, kb, :, :PAIR] += mm(ds, q)
                    part = mm(k_t[heads, keys], ds)
                    dq = part if dq is None else dq + part
                dq_parts.append(dq)
            dq_blocks.append(jnp.concatenate(dq_parts, axis=0) * (HALF**-0.5))
        for qb in range(nblk):
            rows = slice(qb * BLOCK, (qb + 1) * BLOCK)
            qkv_ref[g, rows, :] = jnp.concatenate([dq_blocks[qb].T, s_scr[0, qb]], axis=1).astype(BF16)
        put(g, 0, mm(x_t[...], qkv_ref[g]))
        return carry

    lax.fori_loop(0, pairs, attend_back, 0)

    if linked:
        for n in range(5):
            scatter_small.step(n, 0)
            for p in range(PIECES):
                scatter.step(n, p)

    def dx_copy(i):
        rows = slice(i * BLOCK, (i + 1) * BLOCK)
        return pltpu.make_async_copy(dx_ref.at[rows, :], dx_hbm.at[rows, :], out_sem.at[2, i])

    for qb in range(nblk):
        rows = slice(qb * BLOCK, (qb + 1) * BLOCK)
        total_dx = dx_ref[rows, :]
        for g in range(pairs):
            total_dx = total_dx + mm_nt(qkv_ref[g, rows, :], w_qkv(g))
        dx_ref[rows, :] = total_dx
        dx_copy(qb).start()

    for i in range(nblk):
        for cp in out_copies(pl.ds(i * BLOCK, BLOCK), i):
            cp.wait()
        dx_copy(i).wait()
    if linked:
        gather_small.step(5, 0)
        scatter_small.step(5, 0)
        for p in range(PIECES):
            gather.step(5, p)
            scatter.step(5, p)


def layer(linked, x_in, y_in, lengths, grad_x, grad_y, *rest):
    slots, width = x_in.shape
    ff = 4 * width
    nblk = slots // BLOCK
    pairs = H // 2
    causal = BLOCK * nblk * (nblk + 1) // 2
    vmem = pl.BlockSpec(memory_space=pltpu.VMEM)
    any_ = pl.BlockSpec(memory_space=pl.ANY)
    smem = pl.BlockSpec(memory_space=pltpu.SMEM)
    streams = (
        jax.ShapeDtypeStruct((slots, width), BF16),
        jax.ShapeDtypeStruct((slots, width), F32),
        jax.ShapeDtypeStruct((slots, width), F32),
    )
    wide = (PIECES,) + GRID + (ROWS, CHUNK)
    narrow = (1,) + GRID + (ROWS, PAIR)
    links = []
    if linked:
        outs = [jax.ShapeDtypeStruct(w.shape, F32) for w in rest]
        links += [pltpu.VMEM(wide, BF16), pltpu.VMEM(wide, BF16)]
        links += [pltpu.VMEM(narrow, BF16), pltpu.VMEM(narrow, BF16)]
        for n, _, _, _, _, r, lanes in (wide, narrow):
            links += [
                pltpu.VMEM((n, 4, 2, 2, r, lanes), BF16),
                pltpu.VMEM((n, 2, 4, r, lanes), BF16),
                pltpu.VMEM((n, 4, r, lanes), BF16),
                pltpu.VMEM((n, 3, r, lanes), BF16),
            ]
        for n in (PIECES, 1, PIECES, 1):
            links += [pltpu.SemaphoreType.DMA((n, Z + 3)), pltpu.SemaphoreType.DMA((n, Z + 3))]
        params = pltpu.CompilerParams(
            vmem_limit_bytes=VMEM_LIMIT, collective_id=0, has_side_effects=True
        )
    else:
        outs = [jax.ShapeDtypeStruct(wide, BF16), jax.ShapeDtypeStruct(narrow, BF16)]
        params = pltpu.CompilerParams(vmem_limit_bytes=VMEM_LIMIT)
    return pl.pallas_call(
        functools.partial(layer_kernel, linked),
        out_shape=streams + tuple(outs),
        in_specs=[smem] + [any_] * 4 + [vmem] * len(rest),
        out_specs=(any_,) * 3 + (vmem,) * len(outs),
        scratch_shapes=links
        + [
            pltpu.VMEM((slots, width), BF16),
            pltpu.VMEM((slots, width), F32),
            pltpu.VMEM((slots, width), BF16),
            pltpu.VMEM((slots, width), BF16),
            pltpu.VMEM((slots, width), F32),
            pltpu.VMEM((8, ff), F32),
            pltpu.VMEM((8, ff), F32),
            pltpu.VMEM((pairs, slots, 3 * PAIR), BF16),
            pltpu.VMEM((pairs, PAIR, slots), BF16),
            pltpu.VMEM((slots, width), BF16),
            pltpu.VMEM((pairs, PAIR, slots), BF16),
            pltpu.VMEM((H, causal, BLOCK), BF16),
            pltpu.VMEM((causal, BLOCK), F32),
            pltpu.VMEM((slots, ff), BF16),
            pltpu.VMEM((slots, ff), BF16),
            pltpu.VMEM((slots, width), BF16),
            pltpu.VMEM((slots, width), BF16),
            pltpu.VMEM((width, slots), BF16),
            pltpu.VMEM((2, nblk, BLOCK, BLOCK), F32),
            pltpu.SemaphoreType.DMA((4,)),
            pltpu.SemaphoreType.DMA((3, nblk)),
        ],
        compiler_params=params,
        name="layer",
    )(lengths, x_in, y_in, grad_x, grad_y, *rest)


BOTH = ("dp", "fsdp")


def on_device(
    linked,
    x_in,
    y_in,
    lengths,
    w_qkv,
    w_out,
    gain_one,
    bias_one,
    w_up,
    b_up,
    w_down,
    gain_two,
    bias_two,
    grad_x,
    grad_y,
):
    streams = (x_in, y_in, lengths, grad_x, grad_y)
    width = x_in.shape[1]
    if linked:
        small = jnp.concatenate([gain_one, bias_one, gain_two, bias_two, b_up])
        small = jnp.broadcast_to(small[None], (ROWS, small.shape[0]))
        x_out, y_out, d_x, d_qkv, d_out, d_up, d_down, d_small = layer(
            True, *streams, w_qkv, w_out, w_up, w_down, small
        )
        row = d_small[0]
        vectors = [row[n * ROWS : (n + 1) * ROWS] for n in range(4)] + [row[4 * ROWS :]]
    else:
        blocks = GRID[0] * GRID[1] * GRID[2] * GRID[3]
        pairs = H // 2

        def whole(w):
            return lax.all_gather(w, BOTH, axis=0, tiled=True)

        def cut(w):
            return w.reshape(GRID + (ROWS, CHUNK))

        qkv, out, up, down = (whole(w) for w in (w_qkv, w_out, w_up, w_down))
        pieces = []
        for g in range(pairs):
            lane = [slice(n * width + g * PAIR, n * width + (g + 1) * PAIR) for n in range(3)]
            pieces.append(cut(jnp.concatenate([qkv[:, s] for s in lane] + [out[:, lane[0]]], 1)))
        per = up.shape[1] // CHUNK
        pieces += [cut(up[:, j * CHUNK : (j + 1) * CHUNK]) for j in range(per)]
        down = down.reshape(blocks, per, ROWS, width)
        pieces += [cut(down[:, j].reshape(-1, width)) for j in range(per)]
        vectors = [whole(v) for v in (gain_one, bias_one, gain_two, bias_two, b_up)]
        small = jnp.concatenate([v.reshape(blocks, -1) for v in vectors], axis=1)
        small = jnp.broadcast_to(small[:, None], (blocks, ROWS, small.shape[1]))
        x_out, y_out, d_x, grads, d_small = layer(
            False, *streams, jnp.stack(pieces), small.reshape((1,) + GRID + (ROWS, -1))
        )

        def share(w):
            return lax.psum_scatter(w, BOTH, scatter_dimension=0, tiled=True)

        grads = grads.astype(F32).reshape(PIECES, -1, CHUNK)
        d_qkv = grads[:pairs, :, : 3 * PAIR].reshape(pairs, width, 3, PAIR)
        d_qkv = share(d_qkv.transpose(1, 2, 0, 3).reshape(width, 3 * width))
        d_out = share(grads[:pairs, :, 3 * PAIR :].transpose(1, 0, 2).reshape(width, width))
        d_up = share(grads[pairs : pairs + per].transpose(1, 0, 2).reshape(width, -1))
        d_down = grads[pairs + per :].reshape(per, blocks, ROWS, width).transpose(1, 0, 2, 3)
        d_down = share(d_down.reshape(-1, width))
        rows = d_small.astype(F32).reshape(blocks, ROWS, -1)[:, 0]
        vectors = [share(rows[:, n * ROWS : (n + 1) * ROWS].reshape(-1)) for n in range(4)]
        vectors.append(share(rows[:, 4 * ROWS :].reshape(-1)))
    return (
        x_out,
        y_out,
        d_x,
        d_qkv,
        d_out,
        vectors[0],
        vectors[1],
        d_up,
        vectors[4],
        d_down,
        vectors[2],
        vectors[3],
    )


def solution(mesh):
    matrix, vector = P(BOTH, None), P(BOTH)
    linked = mesh.shape["dp"] == Z and mesh.shape["fsdp"] == GRID[1] * GRID[2] * GRID[3]
    return jax.shard_map(
        functools.partial(on_device, linked),
        mesh=mesh,
        in_specs=(matrix,) * 5
        + (vector, vector, matrix, vector, matrix, vector, vector, matrix, matrix),
        out_specs=(matrix,) * 5
        + (vector, vector, matrix, vector, matrix, vector, vector),
        check_vma=False,
    )
```

```python
import functools

import jax
import jax.numpy as jnp
from jax import lax
from jax.experimental import pallas as pl
from jax.experimental.pallas import tpu as pltpu
from jax.sharding import PartitionSpec as P

H = 8
PAIR = 128
HALF = 64
BLOCK = 256
CHUNK = 512
SPAN = 128
GRID = (4, 2, 2, 2)
ROWS = 16
Z = GRID[0]
PIECES = 12
FIRST_PIECE = 0
LAST_PIECE = 3
VMEM_LIMIT = 67000000
EPSILON = 1e-05
NEGATIVE = -1e30
GELU_C = 0.7978845608028654
GELU_K = 0.044715
F32 = jnp.float32
BF16 = jnp.bfloat16
MESH = pl.DeviceIdType.MESH


def mm(a, b):
    return lax.dot_general(a, b, (((1,), (0,)), ((), ())), preferred_element_type=F32)


def mm_nt(a, b):
    return lax.dot_general(a, b, (((1,), (1,)), ((), ())), preferred_element_type=F32)


def mm_tn(a, b):
    return lax.dot_general(a, b, (((0,), (0,)), ((), ())), preferred_element_type=F32)


def interleave(parts):
    while parts:
        for part in list(parts):
            try:
                next(part)
            except StopIteration:
                parts.remove(part)


class Place:
    def __init__(self):
        self.z = lax.axis_index("dp")
        inner = lax.axis_index("fsdp")
        self.c = lax.rem(inner, 2)
        self.x = lax.rem(inner // 2, 2)
        self.y = inner // 4

    def device(self, z, y, x, c):
        return (z, (y * 2 + x) * 2 + c)

    def first(self, p):
        odd = p % 2
        return (self.y + odd) % 2, (self.x + 1 - odd) % 2

    def second(self, p):
        odd = p % 2
        return (self.y + 1 - odd) % 2, (self.x + odd) % 2

    def around(self, d):
        return lax.rem(self.z + d, Z)


class Gather:
    def __init__(self, place, buf, send, recv):
        self.at, self.buf, self.send, self.recv = place, buf, send, recv

    def copy(self, block, target, p, n):
        ref = self.buf.at[block]
        return pltpu.make_async_remote_copy(
            src_ref=ref,
            dst_ref=ref,
            send_sem=self.send.at[p, n],
            recv_sem=self.recv.at[p, n],
            device_id=target,
            device_id_type=MESH,
        )

    def along_z(self, p, d, source):
        a = self.at
        return self.copy((p, source, a.y, a.x, a.c), a.device(a.around(d), a.y, a.x, a.c), p, d - 1)

    def plane(self, p, n, y, x, to):
        a = self.at
        return self.copy((p, slice(None), y, x, a.c), a.device(a.z, to[0], to[1], a.c), p, n)

    def core(self, p, c):
        a = self.at
        every = slice(None)
        return self.copy((p, every, every, every, c), a.device(a.z, a.y, a.x, 1 - a.c), p, Z + 2)

    def straight(self, p):
        return isinstance(p, int) and p == FIRST_PIECE and self.buf.shape[0] == PIECES

    def step(self, n, p):
        a = self.at
        y1, x1 = a.first(p)
        y2, x2 = a.second(p)
        across = (1 - a.y, 1 - a.x)
        if n == 0:
            for d in range(1, Z):
                self.along_z(p, d, a.z).start()
        elif self.straight(p) and n in (1, 2, 3, 5):
            if n == 1:
                for d in range(1, Z):
                    self.along_z(p, d, a.around(Z - d)).wait_recv()
            trips = ((Z + 1, across), (Z - 1, (y1, x1)), (Z, (y2, x2)))
            for k, to in trips:
                if n == 1:
                    self.plane(p, k, a.y, a.x, to).start()
                elif n == 3:
                    self.plane(p, k, to[0], to[1], to).wait_recv()
                elif n == 5:
                    self.plane(p, k, a.y, a.x, to).wait_send()
            if n == 3:
                self.core(p, a.c).start()
            elif n == 5:
                for d in range(1, Z):
                    self.along_z(p, d, a.z).wait_send()
                self.core(p, a.c).wait_send()
        elif n == 1:
            for d in range(1, Z):
                self.along_z(p, d, a.around(Z - d)).wait_recv()
            self.plane(p, Z - 1, a.y, a.x, (y1, x1)).start()
            self.plane(p, Z, a.y, a.x, (y2, x2)).start()
        elif n == 2:
            self.plane(p, Z - 1, y1, x1, (y1, x1)).wait_recv()
            self.plane(p, Z + 1, y1, x1, (y2, x2)).start()
        elif n == 3:
            self.plane(p, Z, y2, x2, (y2, x2)).wait_recv()
            self.plane(p, Z + 1, 1 - a.y, 1 - a.x, (y2, x2)).wait_recv()
            self.core(p, a.c).start()
        elif n == 4:
            self.core(p, 1 - a.c).wait_recv()
        else:
            for d in range(1, Z):
                self.along_z(p, d, a.z).wait_send()
            self.plane(p, Z - 1, a.y, a.x, (y1, x1)).wait_send()
            self.plane(p, Z, a.y, a.x, (y2, x2)).wait_send()
            self.plane(p, Z + 1, y1, x1, (y2, x2)).wait_send()
            self.core(p, a.c).wait_send()


class Scatter:
    def __init__(self, place, buf, got_core, got_first, got_second, got_z, send, recv, finish):
        self.at, self.buf = place, buf
        self.got_core, self.got_first = got_core, got_first
        self.got_second, self.got_z = got_second, got_z
        self.send, self.recv, self.finish = send, recv, finish

    def copy(self, src, dst, target, p, n):
        return pltpu.make_async_remote_copy(
            src_ref=src,
            dst_ref=dst,
            send_sem=self.send.at[p, n],
            recv_sem=self.recv.at[p, n],
            device_id=target,
            device_id_type=MESH,
        )

    def core(self, p):
        a = self.at
        every = slice(None)
        return self.copy(
            self.buf.at[p, every, every, every, 1 - a.c],
            self.got_core.at[p],
            a.device(a.z, a.y, a.x, 1 - a.c),
            p,
            0,
        )

    def plane(self, p, n, y, x, to):
        a = self.at
        dst = self.got_second.at[p] if n == 3 else self.got_first.at[p, n - 1]
        target = a.device(a.z, to[0], to[1], a.c)
        return self.copy(self.buf.at[p, :, y, x, a.c], dst, target, p, n)

    def along_z(self, p, d):
        a = self.at
        z = a.around(d)
        return self.copy(
            self.buf.at[p, z, a.y, a.x, a.c],
            self.got_z.at[p, d - 1],
            a.device(z, a.y, a.x, a.c),
            p,
            3 + d,
        )

    def add(self, block, value):
        self.buf[block] = (self.buf[block].astype(F32) + value.astype(F32)).astype(BF16)

    def step(self, n, p):
        a = self.at
        y1, x1 = a.first(p)
        y2, x2 = a.second(p)
        every = slice(None)
        across = (1 - a.y, 1 - a.x)
        if n == 0:
            self.core(p).start()
        elif isinstance(p, int) and p == LAST_PIECE and n in (1, 2, 3, 5):
            if n == 1:
                self.core(p).wait_recv()
                self.add((p, every, every, every, a.c), self.got_core[p])
            for k, to in ((1, across), (2, (y1, x1)), (3, (y2, x2))):
                if n == 1:
                    self.plane(p, k, to[0], to[1], to).start()
                elif n == 3:
                    self.plane(p, k, to[0], to[1], to).wait_recv()
                elif n == 5:
                    self.plane(p, k, to[0], to[1], to).wait_send()
            if n == 3:
                total = self.buf[p, :, a.y, a.x, a.c].astype(F32) + self.got_first[p, 0].astype(F32)
                total = total + self.got_first[p, 1].astype(F32) + self.got_second[p].astype(F32)
                self.buf[p, :, a.y, a.x, a.c] = total.astype(BF16)
            for d in range(1, Z):
                if n == 3:
                    self.along_z(p, d).start()
                elif n == 5:
                    self.along_z(p, d).wait_send()
            if n == 5:
                self.core(p).wait_send()
        elif n == 1:
            self.core(p).wait_recv()
            self.add((p, every, every, every, a.c), self.got_core[p])
            self.plane(p, 1, 1 - a.y, 1 - a.x, (y1, x1)).start()
            self.plane(p, 2, y1, x1, (y1, x1)).start()
        elif n == 2:
            self.plane(p, 1, 1 - a.y, 1 - a.x, (y1, x1)).wait_recv()
            self.add((p, every, y2, x2, a.c), self.got_first[p, 0])
            self.plane(p, 3, y2, x2, (y2, x2)).start()
            self.plane(p, 2, y1, x1, (y1, x1)).wait_recv()
            self.add((p, every, a.y, a.x, a.c), self.got_first[p, 1])
        elif n == 3:
            self.plane(p, 3, y2, x2, (y2, x2)).wait_recv()
            self.add((p, every, a.y, a.x, a.c), self.got_second[p])
            for d in range(1, Z):
                self.along_z(p, d).start()
        elif n == 4:
            total = self.buf[p, a.z, a.y, a.x, a.c].astype(F32)
            for d in range(1, Z):
                self.along_z(p, d).wait_recv()
                total = total + self.got_z[p, d - 1].astype(F32)
            self.finish(p, total)
        else:
            self.core(p).wait_send()
            self.plane(p, 1, 1 - a.y, 1 - a.x, (y1, x1)).wait_send()
            self.plane(p, 2, y1, x1, (y1, x1)).wait_send()
            self.plane(p, 3, y2, x2, (y2, x2)).wait_send()
            for d in range(1, Z):
                self.along_z(p, d).wait_send()


SMALL = "small"
START_STEPS = (
    ((False, 0, 0), (False, 0, 1), (False, SMALL, 0),),
    (),
    (),
    (),
    (),
    ((False, 1, 0), (False, 2, 0), (False, 1, 1), (False, 0, 2), (False, 0, 3), (False, 1, 2), (False, 1, 3), (False, 0, 4), (False, 0, 5), (False, 3, 0),),
)
ATTEND_STEPS = (
    (((False, 2, 1), (False, 4, 0),), (), ((False, SMALL, 1),), (), (), (),),
    (((False, 1, 4), (False, 1, 5), (False, 2, 2), (False, 2, 3), (False, 0, 6), (False, 0, 7), (False, 3, 1), (False, 4, 1),), (), ((False, SMALL, 2),), (), (), (),),
    (((False, 1, 6), (False, 2, 4), (False, 0, 8), (False, 2, 5), (False, 3, 2), (False, 3, 3), (False, 1, 7), (False, 0, 9), (False, 4, 2),), ((False, 4, 3),), ((False, SMALL, 3),), (), (), (),),
    ((), ((False, 2, 6), (False, 1, 8), (False, 0, 10),), ((False, 3, 4), (False, 3, 5), (False, 2, 7),), ((False, 1, 9), (False, 0, 11),), (), ((False, 4, 4), (False, 4, 5),),),
)
AFTER_ATTEND = ((False, SMALL, 4),)
NORM_STEPS = (
    ((),),
    (((False, 2, 8), (False, 1, 10),),),
    ((),),
    (((False, 3, 6), (False, 1, 11),),),
)
AFTER_NORM = ((False, 3, 7), (False, 2, 9), (False, 4, 6), (False, 4, 7),)
UP_STEPS = (
    (((False, 2, 10),),),
    ((),),
    (((False, 3, 8),),),
    (((False, 3, 9), (False, 2, 11),),),
)
AFTER_UP = ((False, 4, 8), (False, 3, 10), (False, 4, 9), (False, 4, 10), (False, 3, 11), (False, 4, 11),)
AFTER_DOWN = ((True, 0, 0), (True, 0, 1), (True, 0, 2), (True, 0, 3),)
BACK_STEPS = (
    ((), (), (),),
    (((True, 1, 0), (True, 1, 1), (True, 1, 2),), ((True, 1, 3),), (),),
    ((), (), (),),
    ((), (), ((True, 2, 0), (True, 2, 1), (True, 2, 2),),),
)
UP_SUM_STEPS = (
    ((True, 2, 3), (True, 0, 4),),
    ((True, 0, 5),),
    ((True, 1, 4), (True, 0, 6),),
    ((True, 3, 0), (True, 3, 1), (True, 1, 5), (True, 3, 2),),
)
OUT_SUM_STEPS = ((True, SMALL, 0), (True, 3, 3), (True, 1, 6), (True, 0, 7),)
ATTEND_BACK_STEPS = (
    ((), ((True, 2, 4), (True, 1, 7),), ((True, 2, 5),), ((True, 4, 0), (True, SMALL, 1),), ((True, 4, 1), (True, 2, 6), (True, 4, 2),), ((True, 4, 3), (True, 0, 8),),),
    ((), ((True, 3, 4), (True, 3, 5), (True, 1, 8),), ((True, 2, 7), (True, 3, 6),), ((True, SMALL, 2),), (), ((True, 0, 9),),),
    ((), ((True, 4, 4), (True, 1, 9), (True, 4, 5),), ((True, 4, 6), (True, 3, 7), (True, 2, 8),), ((True, SMALL, 3),), (), ((True, 0, 10),),),
    ((), ((True, 1, 10), (True, 4, 7), (True, 2, 9),), ((True, 3, 8),), ((True, SMALL, 4),), (), ((True, 0, 11),),),
)
INPUT_STEPS = (
    (),
    ((True, 1, 11),),
    ((True, 4, 8), (True, 3, 9), (True, 2, 10),),
    ((True, 2, 11),),
)
LAST_STEPS = ((True, 4, 9), (True, 3, 10), (True, 3, 11), (True, 4, 10), (True, 4, 11),)


def piece_at(order):
    if isinstance(order, int):
        return (8, 4, 0)[order // 4] + order % 4
    return jnp.where(order < 4, order + 8, jnp.where(order < 8, order, order - 8))


def as_matrix(value):
    return value.reshape(-1, value.shape[-1])


def layer_kernel(linked, *refs):
    refs = list(refs)

    def take(n):
        out = refs[:n]
        del refs[:n]
        return out

    lengths_ref, x_hbm, y_hbm, gx_hbm, gy_hbm = take(5)
    if linked:
        s_qkv, s_out, s_up, s_down = take(4)
        vectors = take(5)
        xo_hbm, yo_hbm, dx_hbm, shares, o_small = take(5)
        weights, grads, small, g_small = take(4)
        got = take(8)
        sems = take(8)
    else:
        weights, small = take(2)
        xo_hbm, yo_hbm, dx_hbm, grads, g_small = take(5)
    (
        x_ref,
        y_buf,
        gx_buf,
        gy_buf,
        dx_ref,
        params,
        sums,
        kv_ref,
        q_t,
        att_t,
        inverses,
        datt_t,
        probs,
        bias,
        hidden,
        du_ref,
        x_low,
        df_ref,
        x_t,
        s_scr,
        in_sem,
        out_sem,
    ) = refs

    slots, width = x_ref.shape
    nblk = slots // BLOCK
    ff = hidden.shape[1]
    pairs = H // 2
    per = ff // CHUNK

    loads = []
    for n, (src, dst) in enumerate(
        ((x_hbm, x_ref), (y_hbm, y_buf), (gx_hbm, gx_buf), (gy_hbm, gy_buf))
    ):
        cp = pltpu.make_async_copy(src, dst, in_sem.at[n])
        cp.start()
        loads.append(cp)

    if linked:
        place = Place()
        z, y, x, c = place.z, place.y, place.x, place.c
        barrier = pltpu.get_barrier_semaphore()
        partners = [
            place.device(z, y, x, 1 - c),
            place.device(z, y, 1 - x, c),
            place.device(z, 1 - y, x, c),
            place.device(z, 1 - y, 1 - x, c),
        ] + [place.device(place.around(d), y, x, c) for d in range(1, Z)]
        for partner in partners:
            pl.semaphore_signal(barrier, inc=1, device_id=partner, device_id_type=MESH)
        for g in range(pairs):
            lanes = [slice(n * width + g * PAIR, n * width + (g + 1) * PAIR) for n in range(3)]
            own = [s_qkv[:, lane] for lane in lanes] + [s_out[:, lanes[0]]]
            weights[g, z, y, x, c] = jnp.concatenate(own, axis=1)
        for j in range(per):
            weights[pairs + j, z, y, x, c] = s_up[:, j * CHUNK : (j + 1) * CHUNK]
            weights[pairs + per + j, z, y, x, c] = s_down[j * ROWS : (j + 1) * ROWS, :]
        packed = jnp.zeros((ROWS, PAIR), F32)
        at = 0
        for ref in vectors:
            r = ref.shape[0]
            row = jnp.broadcast_to(ref[...].astype(F32).reshape(1, r), (ROWS, r)).astype(BF16)
            column = lax.broadcasted_iota(jnp.int32, (r, PAIR), 1)
            packed += mm(row, (column == lax.broadcasted_iota(jnp.int32, (r, PAIR), 0) + at).astype(BF16))
            at += r
        small[0, z, y, x, c] = packed.astype(BF16)
        pl.semaphore_wait(barrier, len(partners))

        def finish(p, total):
            shares[p] = total

        def finish_small(p, total):
            o_small[...] = total

        gather = Gather(place, weights, sems[0], sems[1])
        gather_small = Gather(place, small, sems[2], sems[3])
        scatter = Scatter(place, grads, *got[:4], sems[4], sems[5], finish)
        scatter_small = Scatter(place, g_small, *got[4:], sems[6], sems[7], finish_small)
    def run_step(scattered, n, order):
        if scattered:
            scatter.step(n, piece_at(order))
        else:
            gather.step(n, order)

    def steps(events):
        if linked:
            for event in events:
                if event[1] == SMALL:
                    (scatter_small if event[0] else gather_small).step(event[2], 0)
                else:
                    run_step(*event)

    def steps_in_loop(i, table, slot):
        if not linked:
            return
        kinds = []
        for row in table:
            for event in row[slot]:
                if event[1] != SMALL and event[:2] not in kinds:
                    kinds.append(event[:2])
        kinds.sort(key=lambda kind: kind[1])
        for kind in kinds:
            columns = [[e[2] for e in row[slot] if e[:2] == kind] for row in table]
            for k in range(max(len(column) for column in columns)):
                have = [j for j, column in enumerate(columns) if len(column) > k]
                order = jnp.int32(columns[have[0]][k])
                wanted = i == have[0]
                for j in have[1:]:
                    order = jnp.where(i == j, columns[j][k], order)
                    wanted = wanted | (i == j)
                if len(have) == len(columns):
                    run_step(*kind, order)
                else:
                    pl.when(wanted)(functools.partial(run_step, *kind, order))
        for j, row in enumerate(table):
            for e in row[slot]:
                if e[1] == SMALL:
                    pl.when(i == j)(functools.partial(steps, (e,)))

    def segments(pos):
        seg = jnp.zeros(pos.shape, jnp.int32)
        end = jnp.int32(0)
        for j in range(lengths_ref.shape[1]):
            end = end + lengths_ref[0, j]
            seg = seg + (end <= pos).astype(jnp.int32)
        return jnp.where(pos < end, seg, -1 - pos), end

    starts = [BLOCK * (qb * (qb + 1) // 2) for qb in range(nblk)]
    steps(START_STEPS[0])
    for qb in range(nblk):
        q_pos = lax.broadcasted_iota(jnp.int32, (1, BLOCK), 1) + qb * BLOCK
        q_seg, total = segments(q_pos)
        for kb in range(qb + 1):
            k_pos = lax.broadcasted_iota(jnp.int32, (BLOCK, 1), 0) + kb * BLOCK
            k_seg, _ = segments(k_pos)
            allowed = k_seg == q_seg
            if kb == qb:
                allowed = allowed & (k_pos <= q_pos)
            at = starts[qb] + kb * BLOCK
            bias[at : at + BLOCK, :] = jnp.where(allowed, 0.0, NEGATIVE).astype(F32)
        steps(START_STEPS[1 + qb])

    loads[0].wait()
    x_t[...] = x_ref[...].T

    def spread(first, at, r):
        rows = first.shape[0]
        column = lax.broadcasted_iota(jnp.int32, (PAIR, width), 1)
        pick = (lax.broadcasted_iota(jnp.int32, (PAIR, width), 0) == at + column % r).astype(BF16)
        own = lax.broadcasted_iota(jnp.int32, (rows, width), 0)
        mine = own == (lax.broadcasted_iota(jnp.int32, (rows, width), 1) // r) * ROWS
        return jnp.sum(jnp.where(mine, mm(first, pick), 0.0), axis=0, keepdims=True)

    def w_qkv(g):
        return as_matrix(weights[g, ..., : 3 * PAIR])

    def w_out():
        return jnp.concatenate(
            [as_matrix(weights[g, ..., 3 * PAIR :]) for g in range(pairs)], axis=1
        )

    def w_up(j):
        return as_matrix(weights[pairs + j])

    def w_down(j):
        parts = [weights[pairs + per + n, j].reshape(-1, ROWS, width) for n in range(per)]
        return as_matrix(jnp.stack(parts, axis=1))

    steps(START_STEPS[1 + nblk])

    def across(kb, qb):
        at = BLOCK * (kb * nblk - kb * (kb - 1) // 2 + qb - kb)
        return slice(at, at + BLOCK)

    def seen_by(kb):
        return slice(across(kb, kb).start, across(kb, nblk - 1).stop)

    def half_rows(value, a):
        own = value[a * HALF : (a + 1) * HALF]
        rest = jnp.zeros_like(own)
        return jnp.concatenate([rest, own] if a else [own, rest], axis=0)

    def attend(g, carry):
        steps_in_loop(g, ATTEND_STEPS, 0)
        weights_g = w_qkv(g)
        for qb in range(nblk):
            rows = slice(qb * BLOCK, (qb + 1) * BLOCK)
            kv_ref[g, rows, :] = mm(x_ref[rows, :], weights_g[:, PAIR:]).astype(BF16)
        q = mm_tn(weights_g[:, :PAIR], x_t[...]).astype(BF16).astype(F32)
        q_t[g] = (q * (HALF**-0.5)).astype(BF16)
        v_t = kv_ref[g, :, PAIR:].T
        steps_in_loop(g, ATTEND_STEPS, 1)

        def scores(unit, buf):
            qb, a = unit
            nk = (qb + 1) * BLOCK
            part = mm(kv_ref[g, :nk, :PAIR], half_rows(q_t[g, :, qb * BLOCK : nk], a))
            s_scr[buf, : qb + 1] = part.reshape(qb + 1, BLOCK, BLOCK)
            yield

        def masked(unit, buf, r):
            at = starts[unit[0]] + r
            return s_scr[buf, r // BLOCK, r % BLOCK : r % BLOCK + SPAN] + bias[at : at + SPAN, :]

        def soften(unit, buf):
            qb, a = unit
            top = None
            for r in range(0, (qb + 1) * BLOCK, SPAN):
                high = jnp.max(masked(unit, buf, r).reshape(-1, 8, BLOCK), axis=0)
                top = high if top is None else jnp.maximum(top, high)
                yield
            top = jnp.max(top, axis=0, keepdims=True)
            whole = None
            for r in range(0, (qb + 1) * BLOCK, SPAN):
                e = jnp.exp(masked(unit, buf, r) - top)
                one = jnp.sum(e.reshape(-1, 8, BLOCK), axis=0)
                whole = one if whole is None else whole + one
                lanes = across(r // BLOCK, qb)
                probs[2 * g + a, r % BLOCK : r % BLOCK + SPAN, lanes] = e.astype(BF16)
                yield
            whole = jnp.sum(whole, axis=0, keepdims=True)
            inverses[2 * g + a, :, qb * BLOCK : (qb + 1) * BLOCK] = 1.0 / whole

        def mix(unit):
            qb, a = unit
            rows = slice(qb * BLOCK, (qb + 1) * BLOCK)
            heads = slice(a * HALF, (a + 1) * HALF)
            out = None
            for kb in range(qb + 1):
                keys = slice(kb * BLOCK, (kb + 1) * BLOCK)
                part = mm(v_t[heads, keys], probs[2 * g + a, :, across(kb, qb)])
                out = part if out is None else out + part
                yield
            att_t[g, heads, rows] = (out * inverses[2 * g + a, :, rows]).astype(BF16)

        units = [(qb, a) for qb in range(nblk) for a in range(2)]
        for t in range(len(units) + 2):
            parts = []
            if t < len(units):
                parts.append(scores(units[t], t % 2))
            if 1 <= t <= len(units):
                parts.append(soften(units[t - 1], (t - 1) % 2))
            if t >= 2:
                parts.append(mix(units[t - 2]))
            interleave(parts)
            if t % 2 and t > 1:
                steps_in_loop(g, ATTEND_STEPS, 1 + t // 2)
        return carry

    lax.fori_loop(0, pairs, attend, 0)

    steps(AFTER_ATTEND)
    for cp in loads[1:]:
        cp.wait()

    blocks = as_matrix(small[0])
    for n in range(4):
        params[n : n + 1, :width] = spread(blocks, n * ROWS, ROWS)
    for j in range(per):
        rows = blocks.shape[0] // per
        params[4:5, j * CHUNK : (j + 1) * CHUNK] = spread(
            blocks[j * rows : (j + 1) * rows], 4 * ROWS, ff * ROWS // width
        )

    sums[...] = jnp.zeros_like(sums)
    gain_one = params[0:1, :width]
    bias_one = params[1:2, :width]
    gain_two = params[2:3, :width]
    bias_two = params[3:4, :width]

    def norm(value):
        mean = jnp.mean(value, axis=1, keepdims=True)
        centred = value - mean
        var = jnp.mean(centred * centred, axis=1, keepdims=True)
        inv = lax.rsqrt(var + EPSILON)
        return centred * inv, inv

    def norm_back(grad, gain, n, inv):
        gn = grad * gain
        m1 = jnp.mean(gn, axis=1, keepdims=True)
        m2 = jnp.mean(gn * n, axis=1, keepdims=True)
        return (gn - m1 - n * m2) * inv

    def add_sum(row, at, value):
        sums[row : row + 1, at : at + value.shape[1]] += jnp.sum(value, axis=0, keepdims=True)

    def out_copies(rows, i):
        return (
            pltpu.make_async_copy(gx_buf.at[rows, :], xo_hbm.at[rows, :], out_sem.at[0, i]),
            pltpu.make_async_copy(y_buf.at[rows, :], yo_hbm.at[rows, :], out_sem.at[1, i]),
        )

    def keep_norm(i, value, inv):
        for n in range(width // BLOCK):
            bias[pl.ds(n * slots + i * BLOCK, BLOCK), :] = value[:, n * BLOCK : (n + 1) * BLOCK]
        wide = jnp.broadcast_to(inv, (BLOCK, PAIR))
        at = pl.multiple_of(width // BLOCK * slots + i * PAIR, PAIR)
        bias[pl.ds(at, PAIR), :PAIR] = wide[:PAIR]
        bias[pl.ds(at, PAIR), PAIR:] = wide[PAIR:]

    def kept_norm(i):
        value = [bias[pl.ds(n * slots + i * BLOCK, BLOCK), :] for n in range(width // BLOCK)]
        at = pl.multiple_of(width // BLOCK * slots + i * PAIR, PAIR)
        inv = [bias[pl.ds(at, PAIR), n * PAIR : n * PAIR + 1] for n in range(BLOCK // PAIR)]
        return jnp.concatenate(value, axis=1), jnp.concatenate(inv, axis=0)

    def first_norm_rows(i, carry):
        rows = pl.ds(pl.multiple_of(i * BLOCK, BLOCK), BLOCK)
        at_tile = att_t[:, :, rows].reshape(width, BLOCK).T
        branch_a = mm(at_tile, w_out())
        n1, inv1 = norm(x_ref[rows, :].astype(F32) + branch_a)
        keep_norm(i, n1, inv1)
        x_low[rows, :] = (n1 * gain_one + bias_one).astype(BF16)
        y_buf[rows, :] += branch_a
        steps_in_loop(i, NORM_STEPS, 0)
        return carry

    lax.fori_loop(0, nblk, first_norm_rows, 0)
    steps(AFTER_NORM)

    def up_rows(i, carry):
        rows = pl.ds(pl.multiple_of(i * BLOCK, BLOCK), BLOCK)
        xl = x_low[rows, :]
        for j in range(per):
            cols = slice(j * CHUNK, (j + 1) * CHUNK)
            u = mm(xl, w_up(j)) + params[4:5, cols]
            u2 = u * u
            t = jnp.tanh(u * (GELU_C + (GELU_C * GELU_K) * u2))
            h = 0.5 + 0.5 * t
            hidden[rows, cols] = (u * h).astype(BF16)
            slope = h + h * (1.0 - h) * (u * (2.0 * GELU_C + (6.0 * GELU_C * GELU_K) * u2))
            du_ref[rows, cols] = slope.astype(BF16)
        steps_in_loop(i, UP_STEPS, 0)
        return carry

    lax.fori_loop(0, nblk, up_rows, 0)
    steps(AFTER_UP)

    def down_rows(i, carry):
        r0 = pl.multiple_of(i * BLOCK, BLOCK)
        rows = pl.ds(r0, BLOCK)
        branch_f = None
        for j in range(per):
            part = mm(hidden[rows, j * CHUNK : (j + 1) * CHUNK], w_down(j))
            branch_f = part if branch_f is None else branch_f + part
        x_mid = kept_norm(i)[0] * gain_one + bias_one
        n2, inv2 = norm(x_mid + branch_f)
        live = (lax.broadcasted_iota(jnp.int32, (BLOCK, width), 0) + r0) < total
        gx = jnp.where(live, gx_buf[rows, :].astype(F32), 0.0)
        gy = jnp.where(live, gy_buf[rows, :].astype(F32), 0.0)
        gx_buf[rows, :] = jnp.where(live, n2 * gain_two + bias_two, 0.0).astype(BF16)
        y_buf[rows, :] = jnp.where(live, y_buf[rows, :] + branch_f, 0.0)
        for cp in out_copies(rows, i):
            cp.start()
        add_sum(3, 0, gx)
        add_sum(2, 0, gx * n2)
        dr2 = norm_back(gx, gain_two, n2, inv2)
        dx_ref[rows, :] = dr2
        df_ref[rows, :] = (dr2 + gy).astype(BF16)
        return carry

    lax.fori_loop(0, nblk, down_rows, 0)

    for j in range(per):
        part = mm_tn(hidden[:, j * CHUNK : (j + 1) * CHUNK], df_ref[...]).astype(BF16)
        part = part.reshape(-1, per, ROWS, width)
        for n in range(per):
            grads[pairs + per + n, j] = part[:, n].reshape(GRID[1:] + (ROWS, width))
    steps(AFTER_DOWN)

    def backward_rows(i, carry):
        r0 = pl.multiple_of(i * BLOCK, BLOCK)
        rows = pl.ds(r0, BLOCK)
        df = df_ref[rows, :]
        dx_mid = dx_ref[rows, :]
        for j in range(per):
            cols = slice(j * CHUNK, (j + 1) * CHUNK)
            du = (mm_nt(df, w_down(j)) * du_ref[rows, cols].astype(F32)).astype(BF16)
            du_ref[rows, cols] = du
            add_sum(4, j * CHUNK, du.astype(F32))
            dx_mid = dx_mid + mm_nt(du, w_up(j))
            if j % 2:
                steps_in_loop(i, BACK_STEPS, j // 2)
        n1, inv1 = kept_norm(i)
        live = (lax.broadcasted_iota(jnp.int32, (BLOCK, width), 0) + r0) < total
        gy = jnp.where(live, gy_buf[rows, :].astype(F32), 0.0)
        add_sum(1, 0, dx_mid)
        add_sum(0, 0, dx_mid * n1)
        dr1 = norm_back(dx_mid, gain_one, n1, inv1)
        dx_ref[rows, :] = dr1
        da = (dr1 + gy).astype(BF16)
        gy_buf[rows, :] = da
        datt_t[:, :, rows] = mm_nt(w_out(), da).astype(BF16).reshape(pairs, PAIR, BLOCK)
        steps_in_loop(i, BACK_STEPS, 2)
        return carry

    lax.fori_loop(0, nblk, backward_rows, 0)

    def put(p, at, value):
        grads[p, ..., at : at + value.shape[1]] = value.astype(BF16).reshape(
            GRID + (ROWS, value.shape[1])
        )

    for j in range(per):
        put(pairs + j, 0, mm_tn(x_low[...], du_ref[:, j * CHUNK : (j + 1) * CHUNK]))
        steps(UP_SUM_STEPS[j])
    part = mm(att_t[...].reshape(width, slots), gy_buf[...])
    for g in range(pairs):
        put(g, 3 * PAIR, part[:, g * PAIR : (g + 1) * PAIR])

    def gathered(row, at, r):
        value = jnp.broadcast_to(row, (row.shape[1] * ROWS // r, width))
        own = lax.broadcasted_iota(jnp.int32, value.shape, 0) // ROWS
        mine = own == lax.broadcasted_iota(jnp.int32, value.shape, 1) // r
        column = lax.broadcasted_iota(jnp.int32, (width, PAIR), 0)
        pick = (lax.broadcasted_iota(jnp.int32, (width, PAIR), 1) == at + column % r).astype(BF16)
        return mm(jnp.where(mine, value, 0.0).astype(BF16), pick)

    rest = [
        gathered(sums[4:5, j * CHUNK : (j + 1) * CHUNK], 4 * ROWS, ff * ROWS // width)
        for j in range(per)
    ]
    rest = jnp.concatenate(rest, axis=0)
    for n in range(4):
        rest = rest + gathered(sums[n : n + 1, :width], n * ROWS, ROWS)
    g_small[0] = rest.astype(BF16).reshape(GRID + (ROWS, PAIR))

    steps(OUT_SUM_STEPS)

    def ds_at(a, kb, qb=None):
        at = (0, nblk, 0, nblk - 2)[kb] * BLOCK
        lanes = slice(at, at + (nblk - kb) * BLOCK)
        if qb is not None:
            lanes = slice(at + (qb - kb) * BLOCK, at + (qb - kb + 1) * BLOCK)
        row = (2 * a + kb // 2) * BLOCK
        return slice(row, row + BLOCK), lanes

    def grads_of(g):
        return pl.ds(pl.multiple_of(g * 3 * PAIR, PAIR), 3 * PAIR)

    def own_lanes(n, a):
        at = 3 * width + (2 * n + a) * PAIR
        return slice(at, at + PAIR)

    lane = lax.broadcasted_iota(jnp.int32, (slots, PAIR), 1)

    def put_halves(n, value):
        value = value.astype(F32)
        du_ref[:, own_lanes(n, 0)] = jnp.where(lane < HALF, value, 0.0).astype(BF16)
        du_ref[:, own_lanes(n, 1)] = jnp.where(lane < HALF, 0.0, value).astype(BF16)

    turned = slice(slots, 2 * slots)
    key_rows, do_rows = BLOCK, BLOCK + PAIR

    def attend_back(g, carry):
        def put_grad(n, block, value):
            rows = slice(block * BLOCK, (block + 1) * BLOCK)
            lanes = pl.ds(pl.multiple_of(g * 3 * PAIR + n * PAIR, PAIR), PAIR)
            du_ref[rows, lanes] = value.astype(BF16)

        hidden[key_rows : key_rows + PAIR, turned] = kv_ref[g, :, :PAIR].T
        for a in range(2):
            heads = slice(a * HALF, (a + 1) * HALF)
            scaled = datt_t[g, heads, :].astype(F32) * inverses[2 * g + a]
            dots = jnp.sum(att_t[g, heads, :].astype(F32) * scaled, axis=0, keepdims=True)
            inverses[2 * g + a] = dots
            hidden[do_rows + a * HALF : do_rows + (a + 1) * HALF, turned] = scaled.astype(BF16)
        put_halves(0, hidden[do_rows : do_rows + PAIR, turned].T)
        put_halves(1, q_t[g].T)
        steps_in_loop(g, ATTEND_BACK_STEPS, 0)

        def through_values(unit, buf):
            qb, a = unit
            nk = (qb + 1) * BLOCK
            do = half_rows(hidden[do_rows : do_rows + PAIR, slots + qb * BLOCK : slots + nk], a)
            s_scr[buf, : qb + 1] = mm(kv_ref[g, :nk, PAIR:], do).reshape(qb + 1, BLOCK, BLOCK)
            yield

        def through_softmax(unit, buf):
            qb, a = unit
            dots = inverses[2 * g + a, :, qb * BLOCK : (qb + 1) * BLOCK]
            for r in range(0, (qb + 1) * BLOCK, SPAN):
                inner = slice(r % BLOCK, r % BLOCK + SPAN)
                p = probs[2 * g + a, inner, across(r // BLOCK, qb)].astype(F32)
                rows, lanes = ds_at(a, r // BLOCK, qb)
                ds = p * (s_scr[buf, r // BLOCK, inner] - dots)
                hidden[rows.start + r % BLOCK : rows.start + r % BLOCK + SPAN, lanes] = ds.astype(BF16)
                yield

        def to_queries(unit, kept):
            qb, a = unit
            out = None
            for kb in range(qb + 1):
                keys = slice(slots + kb * BLOCK, slots + (kb + 1) * BLOCK)
                k = hidden[key_rows + a * HALF : key_rows + (a + 1) * HALF, keys]
                part = mm(k, hidden[ds_at(a, kb, qb)])
                out = part if out is None else out + part
                yield
            kept[unit] = out * (HALF**-0.5)
            if a:
                put_grad(0, qb, jnp.concatenate([kept[qb, 0], kept[qb, 1]], axis=0).T)

        def to_values(unit, kept):
            kb, a = unit
            kept[unit] = mm(probs[2 * g + a, :, seen_by(kb)], du_ref[kb * BLOCK :, own_lanes(0, a)])
            yield
            if a:
                put_grad(2, kb, kept[kb, 0] + kept[kb, 1])

        def to_keys(unit, kept):
            kb, a = unit
            kept[unit] = mm(hidden[ds_at(a, kb)], du_ref[kb * BLOCK :, own_lanes(1, a)])
            yield
            if a:
                put_grad(1, kb, kept[kb, 0] + kept[kb, 1])

        kept = {}, {}, {}
        units = [(qb, a) for qb in reversed(range(nblk)) for a in range(2)]
        for t in range(len(units) + 2):
            parts = []
            if t < len(units):
                parts.append(through_values(units[t], t % 2))
                parts.append(to_values(units[t], kept[0]))
            if 1 <= t <= len(units):
                parts.append(through_softmax(units[t - 1], (t - 1) % 2))
            if t >= 2:
                parts.append(to_queries(units[t - 2], kept[1]))
                parts.append(to_keys(units[t - 2], kept[2]))
            interleave(parts)
            if t % 2 and t > 1:
                steps_in_loop(g, ATTEND_BACK_STEPS, t // 2)
        put(g, 0, mm(x_t[...], du_ref[:, grads_of(g)]))
        steps_in_loop(g, ATTEND_BACK_STEPS, 1 + nblk)
        return carry

    lax.fori_loop(0, pairs, attend_back, 0)

    def dx_copy(i):
        rows = slice(i * BLOCK, (i + 1) * BLOCK)
        return pltpu.make_async_copy(dx_ref.at[rows, :], dx_hbm.at[rows, :], out_sem.at[2, i])

    for qb in range(nblk):
        rows = slice(qb * BLOCK, (qb + 1) * BLOCK)
        total_dx = dx_ref[rows, :]
        for g in range(pairs):
            grad = du_ref[rows, g * 3 * PAIR : (g + 1) * 3 * PAIR]
            total_dx = total_dx + mm_nt(grad, w_qkv(g))
        dx_ref[rows, :] = total_dx
        dx_copy(qb).start()
        steps(INPUT_STEPS[qb])
    steps(LAST_STEPS)
    for i in range(nblk):
        for cp in out_copies(pl.ds(i * BLOCK, BLOCK), i):
            cp.wait()
        dx_copy(i).wait()
    if linked:
        gather_small.step(5, 0)
        scatter_small.step(5, 0)
        for p in range(PIECES):
            gather.step(5, p)
            scatter.step(5, p)


def layer(linked, x_in, y_in, lengths, grad_x, grad_y, *rest):
    slots, width = x_in.shape
    ff = 4 * width
    nblk = slots // BLOCK
    pairs = H // 2
    causal = BLOCK * nblk * (nblk + 1) // 2
    vmem = pl.BlockSpec(memory_space=pltpu.VMEM)
    any_ = pl.BlockSpec(memory_space=pl.ANY)
    smem = pl.BlockSpec(memory_space=pltpu.SMEM)
    streams = (
        jax.ShapeDtypeStruct((slots, width), BF16),
        jax.ShapeDtypeStruct((slots, width), F32),
        jax.ShapeDtypeStruct((slots, width), F32),
    )
    wide = (PIECES,) + GRID + (ROWS, CHUNK)
    narrow = (1,) + GRID + (ROWS, PAIR)
    links = []
    if linked:
        outs = [
            jax.ShapeDtypeStruct((PIECES, ROWS, CHUNK), F32),
            jax.ShapeDtypeStruct((ROWS, PAIR), F32),
        ]
        links += [pltpu.VMEM(wide, BF16), pltpu.VMEM(wide, BF16)]
        links += [pltpu.VMEM(narrow, BF16), pltpu.VMEM(narrow, BF16)]
        for n, _, _, _, _, r, lanes in (wide, narrow):
            links += [
                pltpu.VMEM((n, 4, 2, 2, r, lanes), BF16),
                pltpu.VMEM((n, 2, 4, r, lanes), BF16),
                pltpu.VMEM((n, 4, r, lanes), BF16),
                pltpu.VMEM((n, 3, r, lanes), BF16),
            ]
        for n in (PIECES, 1, PIECES, 1):
            links += [pltpu.SemaphoreType.DMA((n, Z + 3)), pltpu.SemaphoreType.DMA((n, Z + 3))]
        params = pltpu.CompilerParams(
            vmem_limit_bytes=VMEM_LIMIT, collective_id=0, has_side_effects=True
        )
    else:
        outs = [jax.ShapeDtypeStruct(wide, BF16), jax.ShapeDtypeStruct(narrow, BF16)]
        params = pltpu.CompilerParams(vmem_limit_bytes=VMEM_LIMIT)
    return pl.pallas_call(
        functools.partial(layer_kernel, linked),
        out_shape=streams + tuple(outs),
        in_specs=[smem] + [any_] * 4 + [vmem] * len(rest),
        out_specs=(any_,) * 3 + (vmem,) * len(outs),
        scratch_shapes=links
        + [
            pltpu.VMEM((slots, width), BF16),
            pltpu.VMEM((slots, width), F32),
            pltpu.VMEM((slots, width), BF16),
            pltpu.VMEM((slots, width), BF16),
            pltpu.VMEM((slots, width), F32),
            pltpu.VMEM((8, ff), F32),
            pltpu.VMEM((8, ff), F32),
            pltpu.VMEM((pairs, slots, 2 * PAIR), BF16),
            pltpu.VMEM((pairs, PAIR, slots), BF16),
            pltpu.VMEM((pairs, PAIR, slots), BF16),
            pltpu.VMEM((H, 1, slots), F32),
            pltpu.VMEM((pairs, PAIR, slots), BF16),
            pltpu.VMEM((H, BLOCK, causal), BF16),
            pltpu.VMEM((causal, BLOCK), F32),
            pltpu.VMEM((slots, ff), BF16),
            pltpu.VMEM((slots, ff), BF16),
            pltpu.VMEM((slots, width), BF16),
            pltpu.VMEM((slots, width), BF16),
            pltpu.VMEM((width, slots), BF16),
            pltpu.VMEM((2, nblk, BLOCK, BLOCK), F32),
            pltpu.SemaphoreType.DMA((4,)),
            pltpu.SemaphoreType.DMA((3, nblk)),
        ],
        compiler_params=params,
        name="layer",
    )(lengths, x_in, y_in, grad_x, grad_y, *rest)


def deliver_kernel(xo_hbm, yo_hbm, dx_hbm, shares, small, *refs):
    streams, (d_qkv, d_out, d_up, d_down), vectors = refs[:3], refs[3:7], refs[7:12]
    buffers, (load_sem, store_sem) = refs[12:15], refs[15:]
    loads, stores = [], []
    for k in range(4):
        for n, (src, buf, dst) in enumerate(zip((xo_hbm, yo_hbm, dx_hbm), buffers, streams)):
            part = pl.ds(k * (src.shape[0] // 4), src.shape[0] // 4)
            loads.append(pltpu.make_async_copy(src.at[part], buf.at[part], load_sem.at[n, k]))
            stores.append(pltpu.make_async_copy(buf.at[part], dst.at[part], store_sem.at[n, k]))
    for cp in loads:
        cp.start()
    pairs, width = H // 2, d_out.shape[1]
    for g in range(pairs):
        for n in range(3):
            lanes = slice(n * width + g * PAIR, n * width + (g + 1) * PAIR)
            d_qkv[:, lanes] = shares[g, :, n * PAIR : (n + 1) * PAIR]
        d_out[:, g * PAIR : (g + 1) * PAIR] = shares[g, :, 3 * PAIR :]
    per = d_up.shape[1] // CHUNK
    for j in range(per):
        d_up[:, j * CHUNK : (j + 1) * CHUNK] = shares[pairs + j]
        d_down[j * ROWS : (j + 1) * ROWS, :] = shares[pairs + per + j]
    at = 0
    for ref in vectors:
        ref[...] = small[0, at : at + ref.shape[0]]
        at += ref.shape[0]
    for load, store in zip(loads, stores):
        load.wait()
        store.start()
    for store in stores:
        store.wait()


def deliver(streams, shares, small, shapes):
    vmem = pl.BlockSpec(memory_space=pltpu.VMEM)
    any_ = pl.BlockSpec(memory_space=pl.ANY)
    outs = [jax.ShapeDtypeStruct(s.shape, s.dtype) for s in streams]
    outs += [jax.ShapeDtypeStruct(shape, F32) for shape in shapes]
    return pl.pallas_call(
        deliver_kernel,
        out_shape=outs,
        in_specs=[any_] * 3 + [vmem] * 2,
        out_specs=[any_] * 3 + [vmem] * 9,
        scratch_shapes=[pltpu.VMEM(s.shape, s.dtype) for s in streams]
        + [pltpu.SemaphoreType.DMA((3, 4)), pltpu.SemaphoreType.DMA((3, 4))],
        compiler_params=pltpu.CompilerParams(vmem_limit_bytes=VMEM_LIMIT),
        name="deliver",
    )(*streams, shares, small)


BOTH = ("dp", "fsdp")


def on_device(
    linked,
    x_in,
    y_in,
    lengths,
    w_qkv,
    w_out,
    gain_one,
    bias_one,
    w_up,
    b_up,
    w_down,
    gain_two,
    bias_two,
    grad_x,
    grad_y,
):
    streams = (x_in, y_in, lengths, grad_x, grad_y)
    width = x_in.shape[1]
    if linked:
        ends = (gain_one, bias_one, gain_two, bias_two, b_up)
        *out_streams, shares, small = layer(True, *streams, w_qkv, w_out, w_up, w_down, *ends)
        shapes = [w.shape for w in (w_qkv, w_out, w_up, w_down) + ends]
        x_out, y_out, d_x, d_qkv, d_out, d_up, d_down, *vectors = deliver(
            out_streams, shares, small, shapes
        )
    else:
        blocks = GRID[0] * GRID[1] * GRID[2] * GRID[3]
        pairs = H // 2

        def whole(w):
            return lax.all_gather(w, BOTH, axis=0, tiled=True)

        def cut(w):
            return w.reshape(GRID + (ROWS, CHUNK))

        qkv, out, up, down = (whole(w) for w in (w_qkv, w_out, w_up, w_down))
        pieces = []
        for g in range(pairs):
            lane = [slice(n * width + g * PAIR, n * width + (g + 1) * PAIR) for n in range(3)]
            pieces.append(cut(jnp.concatenate([qkv[:, s] for s in lane] + [out[:, lane[0]]], 1)))
        per = up.shape[1] // CHUNK
        pieces += [cut(up[:, j * CHUNK : (j + 1) * CHUNK]) for j in range(per)]
        down = down.reshape(blocks, per, ROWS, width)
        pieces += [cut(down[:, j].reshape(-1, width)) for j in range(per)]
        vectors = [whole(v) for v in (gain_one, bias_one, gain_two, bias_two, b_up)]
        small = jnp.concatenate([v.reshape(blocks, -1) for v in vectors], axis=1)
        small = jnp.broadcast_to(small[:, None], (blocks, ROWS, small.shape[1]))
        x_out, y_out, d_x, grads, d_small = layer(
            False, *streams, jnp.stack(pieces), small.reshape((1,) + GRID + (ROWS, -1))
        )

        def share(w):
            return lax.psum_scatter(w, BOTH, scatter_dimension=0, tiled=True)

        grads = grads.astype(F32).reshape(PIECES, -1, CHUNK)
        d_qkv = grads[:pairs, :, : 3 * PAIR].reshape(pairs, width, 3, PAIR)
        d_qkv = share(d_qkv.transpose(1, 2, 0, 3).reshape(width, 3 * width))
        d_out = share(grads[:pairs, :, 3 * PAIR :].transpose(1, 0, 2).reshape(width, width))
        d_up = share(grads[pairs : pairs + per].transpose(1, 0, 2).reshape(width, -1))
        d_down = grads[pairs + per :].reshape(per, blocks, ROWS, width).transpose(1, 0, 2, 3)
        d_down = share(d_down.reshape(-1, width))
        rows = d_small.astype(F32).reshape(blocks, ROWS, -1)[:, 0]
        vectors = [share(rows[:, n * ROWS : (n + 1) * ROWS].reshape(-1)) for n in range(4)]
        vectors.append(share(rows[:, 4 * ROWS :].reshape(-1)))
    return (
        x_out,
        y_out,
        d_x,
        d_qkv,
        d_out,
        vectors[0],
        vectors[1],
        d_up,
        vectors[4],
        d_down,
        vectors[2],
        vectors[3],
    )


def solution(mesh):
    matrix, vector = P(BOTH, None), P(BOTH)
    linked = mesh.shape["dp"] == Z and mesh.shape["fsdp"] == GRID[1] * GRID[2] * GRID[3]
    return jax.shard_map(
        functools.partial(on_device, linked),
        mesh=mesh,
        in_specs=(matrix,) * 5
        + (vector, vector, matrix, vector, matrix, vector, vector, matrix, matrix),
        out_specs=(matrix,) * 5
        + (vector, vector, matrix, vector, matrix, vector, vector),
        check_vma=False,
    )
```

```python
import functools

import jax
import jax.numpy as jnp
from jax import lax
from jax.experimental import pallas as pl
from jax.experimental.pallas import tpu as pltpu
from jax.sharding import PartitionSpec as P

H = 8
PAIR = 128
HALF = 64
BLOCK = 256
CHUNK = 512
SPAN = 128
GRID = (4, 2, 2, 2)
ROWS = 16
Z = GRID[0]
PIECES = 12
NORM_ROWS = 64
FIRST_PIECE = 0
LAST_PIECE = 3
VMEM_LIMIT = 60000000
DELIVER_LIMIT = 4000000
EPSILON = 1e-05
NEGATIVE = -1e30
GELU_C = 0.7978845608028654
GELU_K = 0.044715
F32 = jnp.float32
BF16 = jnp.bfloat16
MESH = pl.DeviceIdType.MESH


def mm(a, b):
    return lax.dot_general(a, b, (((1,), (0,)), ((), ())), preferred_element_type=F32)


def mm_nt(a, b):
    return lax.dot_general(a, b, (((1,), (1,)), ((), ())), preferred_element_type=F32)


def mm_tn(a, b):
    return lax.dot_general(a, b, (((0,), (0,)), ((), ())), preferred_element_type=F32)


def interleave(parts):
    while parts:
        for part in list(parts):
            try:
                next(part)
            except StopIteration:
                parts.remove(part)


def aligned(value, n):
    return value if isinstance(value, int) else pl.multiple_of(value, n)


def repeat(n, body, unrolled):
    if unrolled:
        for i in range(n):
            body(i, 0)
    else:
        lax.fori_loop(0, n, body, 0)


class Place:
    def __init__(self):
        self.z = lax.axis_index("dp")
        inner = lax.axis_index("fsdp")
        self.c = lax.rem(inner, 2)
        self.x = lax.rem(inner // 2, 2)
        self.y = inner // 4

    def device(self, z, y, x, c):
        return (z, (y * 2 + x) * 2 + c)

    def around(self, d):
        return lax.rem(self.z + d, Z)


LOW, HIGH, EVERY = slice(0, Z // 2), slice(Z // 2, Z), slice(None)


class Gather:
    def __init__(self, place, buf, send, recv, straight=()):
        self.at, self.buf, self.send, self.recv, self.straight = place, buf, send, recv, straight

    def copy(self, block, target, p, n):
        ref = self.buf.at[block]
        return pltpu.make_async_remote_copy(
            src_ref=ref,
            dst_ref=ref,
            send_sem=self.send.at[p, n],
            recv_sem=self.recv.at[p, n],
            device_id=target,
            device_id_type=MESH,
        )

    def along_z(self, p, d, source):
        a = self.at
        return self.copy((p, source, a.y, a.x, a.c), a.device(a.around(d), a.y, a.x, a.c), p, d - 1)

    def plane(self, p, n, zs, y, x, along):
        a = self.at
        ty = a.y if along == "x" else 1 - a.y
        tx = a.x if along == "y" else 1 - a.x
        return self.copy((p, zs, y, x, a.c), a.device(a.z, ty, tx, a.c), p, Z - 1 + n)

    def core(self, p, c):
        a = self.at
        return self.copy((p, EVERY, EVERY, EVERY, c), a.device(a.z, a.y, a.x, 1 - a.c), p, Z + 3)

    def step(self, n, p):
        a = self.at
        y, x = a.y, a.x
        once = isinstance(p, int) and p in self.straight
        if n == 0:
            for d in range(1, Z):
                self.along_z(p, d, a.z).start()
        elif n == 1:
            for d in range(1, Z):
                self.along_z(p, d, a.around(Z - d)).wait_recv()
            if once:
                self.plane(p, 2, EVERY, y, x, "xy").start()
            self.plane(p, 0, EVERY, y, x, "x").start()
            self.plane(p, 1, EVERY, y, x, "y").start()
        elif n == 2 and not once:
            self.plane(p, 0, EVERY, y, 1 - x, "x").wait_recv()
            self.plane(p, 2, LOW, y, 1 - x, "y").start()
            self.plane(p, 1, EVERY, 1 - y, x, "y").wait_recv()
            self.plane(p, 3, HIGH, 1 - y, x, "x").start()
        elif n == 3:
            if once:
                self.plane(p, 0, EVERY, y, 1 - x, "x").wait_recv()
                self.plane(p, 1, EVERY, 1 - y, x, "y").wait_recv()
                self.plane(p, 2, EVERY, 1 - y, 1 - x, "xy").wait_recv()
            else:
                self.plane(p, 2, LOW, 1 - y, 1 - x, "y").wait_recv()
                self.plane(p, 3, HIGH, 1 - y, 1 - x, "x").wait_recv()
            self.core(p, a.c).start()
        elif n == 4:
            self.core(p, 1 - a.c).wait_recv()
        elif n == 5:
            for d in range(1, Z):
                self.along_z(p, d, a.z).wait_send()
            self.plane(p, 0, EVERY, y, x, "x").wait_send()
            self.plane(p, 1, EVERY, y, x, "y").wait_send()
            if once:
                self.plane(p, 2, EVERY, y, x, "xy").wait_send()
            else:
                self.plane(p, 2, LOW, y, 1 - x, "y").wait_send()
                self.plane(p, 3, HIGH, 1 - y, x, "x").wait_send()
            self.core(p, a.c).wait_send()


class Scatter:
    def __init__(self, place, buf, got_core, got_first, got_second, got_z, got_last, send, recv, finish, straight=()):
        self.at, self.buf, self.straight = place, buf, straight
        self.got_core, self.got_first = got_core, got_first
        self.got_second, self.got_z, self.got_last = got_second, got_z, got_last
        self.send, self.recv, self.finish = send, recv, finish

    def copy(self, src, dst, target, p, n):
        return pltpu.make_async_remote_copy(
            src_ref=src,
            dst_ref=dst,
            send_sem=self.send.at[p, n],
            recv_sem=self.recv.at[p, n],
            device_id=target,
            device_id_type=MESH,
        )

    def core(self, p):
        a = self.at
        src = self.buf.at[p, EVERY, EVERY, EVERY, 1 - a.c]
        return self.copy(src, self.got_core.at[p], a.device(a.z, a.y, a.x, 1 - a.c), p, 0)

    def plane(self, p, n):
        a = self.at
        along_x, along_y = a.device(a.z, a.y, 1 - a.x, a.c), a.device(a.z, 1 - a.y, a.x, a.c)
        if n == 1:
            return self.copy(self.buf.at[p, LOW, :, 1 - a.x, a.c], self.got_first.at[p, 0], along_x, p, n)
        if n == 2:
            return self.copy(self.buf.at[p, HIGH, 1 - a.y, :, a.c], self.got_first.at[p, 1], along_y, p, n)
        if n == 3:
            return self.copy(self.buf.at[p, LOW, 1 - a.y, a.x, a.c], self.got_second.at[p, 0], along_y, p, n)
        return self.copy(self.buf.at[p, HIGH, a.y, 1 - a.x, a.c], self.got_second.at[p, 1], along_x, p, n)

    def at_once(self, p, n):
        a = self.at
        y = a.y if n == 1 else 1 - a.y
        x = a.x if n == 2 else 1 - a.x
        target = a.device(a.z, y, x, a.c)
        return self.copy(self.buf.at[p, :, y, x, a.c], self.got_last.at[n - 1], target, p, n)

    def along_z(self, p, d):
        a = self.at
        z = a.around(d)
        target = a.device(z, a.y, a.x, a.c)
        return self.copy(self.buf.at[p, z, a.y, a.x, a.c], self.got_z.at[p, d - 1], target, p, 4 + d)

    def add(self, block, *values):
        total = self.buf[block].astype(F32)
        for value in values:
            total = total + value.astype(F32)
        self.buf[block] = total.astype(BF16)

    def step(self, n, p):
        a = self.at
        once = isinstance(p, int) and p in self.straight
        if n == 0:
            self.core(p).start()
        elif n == 1:
            self.core(p).wait_recv()
            self.add((p, EVERY, EVERY, EVERY, a.c), self.got_core[p])
            for k in (3, 1, 2) if once else (1, 2):
                (self.at_once(p, k) if once else self.plane(p, k)).start()
        elif n == 2 and not once:
            self.plane(p, 1).wait_recv()
            self.add((p, LOW, EVERY, a.x, a.c), self.got_first[p, 0])
            self.plane(p, 3).start()
            self.plane(p, 2).wait_recv()
            self.add((p, HIGH, a.y, EVERY, a.c), self.got_first[p, 1])
            self.plane(p, 4).start()
        elif n == 3:
            own = (p, EVERY, a.y, a.x, a.c)
            if once:
                for k in (1, 2, 3):
                    self.at_once(p, k).wait_recv()
                self.add(own, self.got_last[0], self.got_last[1], self.got_last[2])
            else:
                for k in (3, 4):
                    self.plane(p, k).wait_recv()
                self.add(own, as_matrix(self.got_second[p]).reshape(Z, ROWS, -1))
            for d in range(1, Z):
                self.along_z(p, d).start()
        elif n == 4:
            total = self.buf[p, a.z, a.y, a.x, a.c].astype(F32)
            for d in range(1, Z):
                self.along_z(p, d).wait_recv()
                total = total + self.got_z[p, d - 1].astype(F32)
            self.finish(p, total)
        elif n == 5:
            self.core(p).wait_send()
            for k in (1, 2, 3) if once else (1, 2, 3, 4):
                (self.at_once(p, k) if once else self.plane(p, k)).wait_send()
            for d in range(1, Z):
                self.along_z(p, d).wait_send()


SMALL = "small"
START_STEPS = (
    ((False, 0, 0), (False, 0, 1), (False, 0, 2), (False, 0, 3), (False, SMALL, 0),),
    (),
    (),
    (),
    (),
    ((False, 1, 0), (False, 2, 0), (False, 0, 4), (False, 1, 1), (False, 0, 5), (False, 1, 2), (False, 0, 6), (False, 1, 3), (False, 0, 7), (False, 3, 0),),
)
ATTEND_STEPS = (
    (((False, 1, 4), (False, 0, 8), (False, 4, 0), (False, 2, 1),), ((False, 1, 5), (False, 0, 9),), ((False, 2, 2), (False, SMALL, 1),), ((False, 1, 6), (False, 0, 10),), (), ((False, 2, 3),),),
    (((False, 2, 4), (False, 3, 1), (False, 1, 7), (False, 0, 11), (False, 4, 1), (False, 2, 5),), ((False, 3, 2), (False, 1, 8),), ((False, SMALL, 2),), (), ((False, 4, 2), (False, 2, 6),), ((False, 3, 3), (False, 1, 9),),),
    ((), ((False, 3, 4), (False, 1, 10),), ((False, 4, 3), (False, SMALL, 3),), ((False, 2, 7),), ((False, 4, 4), (False, 3, 5), (False, 1, 11),), (),),
    ((), ((False, 4, 5), (False, 2, 8), (False, 3, 6),), (), (), ((False, 4, 6), (False, 2, 9),), (),),
)
AFTER_ATTEND = ((False, SMALL, 4),)
NORM_STEPS = (
    (((False, 2, 10),),),
    (((False, 3, 7),),),
    ((),),
    (((False, 4, 7), (False, 2, 11),),),
)
AFTER_NORM = ()
UP_STEPS = (
    (((False, 3, 8), (False, 3, 9),),),
    (((False, 3, 10),),),
    (((False, 4, 8), (False, 4, 9), (False, 3, 11), (False, 4, 10),),),
    ((),),
)
AFTER_UP = ((False, 4, 11),)
AFTER_DOWN = ((True, 0, 0), (True, 0, 1), (True, 0, 2), (True, 0, 3),)
BACK_STEPS = (
    ((), (), ((True, 1, 0),),),
    (((True, 1, 1), (True, 1, 2),), ((True, 1, 3),), (),),
    ((), (), ((True, 2, 0),),),
    ((), ((True, 2, 1),), ((True, 2, 2),),),
)
UP_SUM_STEPS = (
    ((True, 0, 4),),
    ((True, 2, 3), (True, 3, 0), (True, 0, 5),),
    ((True, 0, 6),),
    ((True, 3, 1), (True, 1, 4), (True, 0, 7),),
)
OUT_SUM_STEPS = ((True, SMALL, 0), (True, 3, 2), (True, 1, 5), (True, 1, 6),)
ATTEND_BACK_STEPS = (
    (((True, 3, 3),), ((True, 4, 0), (True, 1, 7),), ((True, 2, 4), (True, 4, 1),), ((True, SMALL, 1),), ((True, 2, 5), (True, 4, 2),), ((True, 0, 8),),),
    (((True, 2, 6),), ((True, 4, 3), (True, 2, 7),), ((True, 3, 4), (True, 3, 5), (True, 1, 8),), ((True, SMALL, 2),), ((True, 3, 6),), ((True, 0, 9),),),
    ((), ((True, 3, 7),), ((True, 4, 4), (True, 2, 8), (True, 1, 9),), ((True, SMALL, 3),), ((True, 4, 5),), ((True, 0, 10),),),
    (((True, 4, 6),), ((True, 4, 7), (True, 3, 8),), ((True, 1, 10), (True, 2, 9),), ((True, SMALL, 4),), (), ((True, 0, 11),),),
)
INPUT_STEPS = (
    ((True, 4, 8),),
    ((True, 2, 10), (True, 1, 11), (True, 3, 9),),
    ((True, 2, 11),),
    (),
)
LAST_STEPS = ((True, 3, 10), (True, 4, 9), (True, 3, 11), (True, 4, 10), (True, 4, 11),)


def piece_at(order):
    if isinstance(order, int):
        return (8, 4, 0)[order // 4] + order % 4
    return jnp.where(order < 4, order + 8, jnp.where(order < 8, order, order - 8))


def as_matrix(value):
    return value.reshape(-1, value.shape[-1])


def layer_kernel(linked, *refs):
    refs = list(refs)

    def take(n):
        out = refs[:n]
        del refs[:n]
        return out

    lengths_ref, x_hbm, y_hbm, gx_hbm, gy_hbm = take(5)
    if linked:
        s_qkv, s_out, s_up, s_down = take(4)
        vectors = take(5)
        gx_buf, y_buf, dx_ref, shares, o_small = take(5)
        weights, grads, small, g_small = take(4)
        got = take(10)
        sems = take(8)
    else:
        weights, small = take(2)
        gx_buf, y_buf, dx_ref, grads, g_small = take(5)
    (
        x_ref,
        gy_buf,
        params,
        sums,
        kv_ref,
        q_t,
        att_t,
        inverses,
        datt_t,
        probs,
        bias,
        hidden,
        du_ref,
        x_low,
        df_ref,
        x_t,
        s_scr,
        in_sem,
    ) = refs

    slots, width = x_ref.shape
    nblk = slots // BLOCK
    ff = hidden.shape[1]
    pairs = H // 2
    per = ff // CHUNK

    loads = []
    for n, (src, dst) in enumerate(
        ((x_hbm, x_ref), (y_hbm, y_buf), (gx_hbm, gx_buf), (gy_hbm, gy_buf))
    ):
        cp = pltpu.make_async_copy(src, dst, in_sem.at[n])
        cp.start()
        loads.append(cp)

    if linked:
        place = Place()
        z, y, x, c = place.z, place.y, place.x, place.c
        barrier = pltpu.get_barrier_semaphore()
        partners = [
            place.device(z, y, x, 1 - c),
            place.device(z, y, 1 - x, c),
            place.device(z, 1 - y, x, c),
            place.device(z, 1 - y, 1 - x, c),
        ] + [place.device(place.around(d), y, x, c) for d in range(1, Z)]
        for partner in partners:
            pl.semaphore_signal(barrier, inc=1, device_id=partner, device_id_type=MESH)
        for g in range(pairs):
            lanes = [slice(n * width + g * PAIR, n * width + (g + 1) * PAIR) for n in range(3)]
            own = [s_qkv[:, lane] for lane in lanes] + [s_out[:, lanes[0]]]
            weights[g, z, y, x, c] = jnp.concatenate(own, axis=1)
        for j in range(per):
            weights[pairs + j, z, y, x, c] = s_up[:, j * CHUNK : (j + 1) * CHUNK]
            weights[pairs + per + j, z, y, x, c] = s_down[j * ROWS : (j + 1) * ROWS, :]
        packed = jnp.zeros((ROWS, PAIR), F32)
        at = 0
        for ref in vectors:
            r = ref.shape[0]
            row = jnp.broadcast_to(ref[...].astype(F32).reshape(1, r), (ROWS, r)).astype(BF16)
            column = lax.broadcasted_iota(jnp.int32, (r, PAIR), 1)
            packed += mm(row, (column == lax.broadcasted_iota(jnp.int32, (r, PAIR), 0) + at).astype(BF16))
            at += r
        small[0, z, y, x, c] = packed.astype(BF16)
        pl.semaphore_wait(barrier, len(partners))

        def finish(p, total):
            shares[p] = total

        def finish_small(p, total):
            o_small[...] = total

        gather = Gather(place, weights, sems[0], sems[1], (FIRST_PIECE,))
        gather_small = Gather(place, small, sems[2], sems[3])
        scatter = Scatter(place, grads, *got[:5], sems[4], sems[5], finish, (LAST_PIECE,))
        scatter_small = Scatter(place, g_small, *got[5:], sems[6], sems[7], finish_small)
    def run_step(scattered, n, order):
        if scattered:
            scatter.step(n, piece_at(order))
        else:
            gather.step(n, order)

    def steps(events):
        if linked:
            for event in events:
                if event[1] == SMALL:
                    (scatter_small if event[0] else gather_small).step(event[2], 0)
                else:
                    run_step(*event)

    def steps_in_loop(i, table, slot):
        if not linked:
            return
        if isinstance(i, int):
            steps(table[i][slot])
            return
        kinds = []
        for row in table:
            for event in row[slot]:
                if event[1] != SMALL and event[:2] not in kinds:
                    kinds.append(event[:2])
        kinds.sort(key=lambda kind: kind[1])
        for kind in kinds:
            columns = [[e[2] for e in row[slot] if e[:2] == kind] for row in table]
            for k in range(max(len(column) for column in columns)):
                have = [j for j, column in enumerate(columns) if len(column) > k]
                order = jnp.int32(columns[have[0]][k])
                wanted = i == have[0]
                for j in have[1:]:
                    order = jnp.where(i == j, columns[j][k], order)
                    wanted = wanted | (i == j)
                if len(have) == len(columns):
                    run_step(*kind, order)
                else:
                    pl.when(wanted)(functools.partial(run_step, *kind, order))
        for j, row in enumerate(table):
            for e in row[slot]:
                if e[1] == SMALL:
                    pl.when(i == j)(functools.partial(steps, (e,)))

    def segments(pos):
        seg = jnp.zeros(pos.shape, jnp.int32)
        end = jnp.int32(0)
        for j in range(lengths_ref.shape[1]):
            end = end + lengths_ref[0, j]
            seg = seg + (end <= pos).astype(jnp.int32)
        return jnp.where(pos < end, seg, -1 - pos), end

    starts = [BLOCK * (qb * (qb + 1) // 2) for qb in range(nblk)]
    steps(START_STEPS[0])
    for qb in range(nblk):
        q_pos = lax.broadcasted_iota(jnp.int32, (1, BLOCK), 1) + qb * BLOCK
        q_seg, total = segments(q_pos)
        for kb in range(qb + 1):
            k_pos = lax.broadcasted_iota(jnp.int32, (BLOCK, 1), 0) + kb * BLOCK
            k_seg, _ = segments(k_pos)
            allowed = k_seg == q_seg
            if kb == qb:
                allowed = allowed & (k_pos <= q_pos)
            at = starts[qb] + kb * BLOCK
            bias[at : at + BLOCK, :] = jnp.where(allowed, 0.0, NEGATIVE).astype(F32)
        steps(START_STEPS[1 + qb])

    loads[0].wait()
    x_t[...] = x_ref[...].T

    def spread(first, at, r):
        rows = first.shape[0]
        column = lax.broadcasted_iota(jnp.int32, (PAIR, width), 1)
        pick = (lax.broadcasted_iota(jnp.int32, (PAIR, width), 0) == at + column % r).astype(BF16)
        own = lax.broadcasted_iota(jnp.int32, (rows, width), 0)
        mine = own == (lax.broadcasted_iota(jnp.int32, (rows, width), 1) // r) * ROWS
        return jnp.sum(jnp.where(mine, mm(first, pick), 0.0), axis=0, keepdims=True)

    def w_qkv(g):
        return as_matrix(weights[g, ..., : 3 * PAIR])

    def w_out():
        return jnp.concatenate(
            [as_matrix(weights[g, ..., 3 * PAIR :]) for g in range(pairs)], axis=1
        )

    def w_up(j):
        return as_matrix(weights[pairs + j])

    def w_down(j):
        parts = [weights[pairs + per + n, j].reshape(-1, ROWS, width) for n in range(per)]
        return as_matrix(jnp.stack(parts, axis=1))

    steps(START_STEPS[1 + nblk])

    def across(kb, qb):
        at = BLOCK * (kb * nblk - kb * (kb - 1) // 2 + qb - kb)
        return slice(at, at + BLOCK)

    def seen_by(kb):
        return slice(across(kb, kb).start, across(kb, nblk - 1).stop)

    def half_rows(value, a):
        own = value[a * HALF : (a + 1) * HALF]
        rest = jnp.zeros_like(own)
        return jnp.concatenate([rest, own] if a else [own, rest], axis=0)

    def attend(g, carry):
        steps_in_loop(g, ATTEND_STEPS, 0)
        weights_g = w_qkv(g)
        for qb in range(nblk):
            rows = slice(qb * BLOCK, (qb + 1) * BLOCK)
            kv_ref[g, rows, :] = mm(x_ref[rows, :], weights_g[:, PAIR:]).astype(BF16)
        q = mm_tn(weights_g[:, :PAIR], x_t[...]).astype(BF16).astype(F32)
        q_t[g] = (q * (HALF**-0.5)).astype(BF16)
        v_t = kv_ref[g, :, PAIR:].T
        steps_in_loop(g, ATTEND_STEPS, 1)

        def scores(unit, buf):
            qb, a = unit
            nk = (qb + 1) * BLOCK
            part = mm(kv_ref[g, :nk, :PAIR], half_rows(q_t[g, :, qb * BLOCK : nk], a))
            s_scr[buf, : qb + 1] = part.reshape(qb + 1, BLOCK, BLOCK)
            yield

        def masked(unit, buf, r):
            at = starts[unit[0]] + r
            return s_scr[buf, r // BLOCK, r % BLOCK : r % BLOCK + SPAN] + bias[at : at + SPAN, :]

        def soften(unit, buf):
            qb, a = unit
            top = None
            for r in range(0, (qb + 1) * BLOCK, SPAN):
                high = jnp.max(masked(unit, buf, r).reshape(-1, 8, BLOCK), axis=0)
                top = high if top is None else jnp.maximum(top, high)
                yield
            top = jnp.max(top, axis=0, keepdims=True)
            whole = None
            for r in range(0, (qb + 1) * BLOCK, SPAN):
                e = jnp.exp(masked(unit, buf, r) - top)
                one = jnp.sum(e.reshape(-1, 8, BLOCK), axis=0)
                whole = one if whole is None else whole + one
                lanes = across(r // BLOCK, qb)
                probs[2 * g + a, r % BLOCK : r % BLOCK + SPAN, lanes] = e.astype(BF16)
                yield
            whole = jnp.sum(whole, axis=0, keepdims=True)
            inverses[2 * g + a, :, qb * BLOCK : (qb + 1) * BLOCK] = 1.0 / whole

        def mix(unit):
            qb, a = unit
            rows = slice(qb * BLOCK, (qb + 1) * BLOCK)
            heads = slice(a * HALF, (a + 1) * HALF)
            out = None
            for kb in range(qb + 1):
                keys = slice(kb * BLOCK, (kb + 1) * BLOCK)
                part = mm(v_t[heads, keys], probs[2 * g + a, :, across(kb, qb)])
                out = part if out is None else out + part
                yield
            att_t[g, heads, rows] = (out * inverses[2 * g + a, :, rows]).astype(BF16)

        units = [(qb, a) for qb in range(nblk) for a in range(2)]
        for t in range(len(units) + 2):
            parts = []
            if t < len(units):
                parts.append(scores(units[t], t % 2))
            if 1 <= t <= len(units):
                parts.append(soften(units[t - 1], (t - 1) % 2))
            if t >= 2:
                parts.append(mix(units[t - 2]))
            interleave(parts)
            if t % 2 and t > 1:
                steps_in_loop(g, ATTEND_STEPS, 1 + t // 2)
        return carry

    repeat(pairs, attend, False)

    steps(AFTER_ATTEND)
    for cp in loads[1:]:
        cp.wait()

    blocks = as_matrix(small[0])
    for n in range(4):
        params[n : n + 1, :width] = spread(blocks, n * ROWS, ROWS)
    for j in range(per):
        rows = blocks.shape[0] // per
        params[4:5, j * CHUNK : (j + 1) * CHUNK] = spread(
            blocks[j * rows : (j + 1) * rows], 4 * ROWS, ff * ROWS // width
        )

    sums[...] = jnp.zeros_like(sums)
    gain_one = params[0:1, :width]
    bias_one = params[1:2, :width]
    gain_two = params[2:3, :width]
    bias_two = params[3:4, :width]

    def norm(value):
        mean = jnp.mean(value, axis=1, keepdims=True)
        centred = value - mean
        var = jnp.mean(centred * centred, axis=1, keepdims=True)
        inv = lax.rsqrt(var + EPSILON)
        return centred * inv, inv

    def norm_back(grad, gain, n, inv):
        gn = grad * gain
        m1 = jnp.mean(gn, axis=1, keepdims=True)
        m2 = jnp.mean(gn * n, axis=1, keepdims=True)
        return (gn - m1 - n * m2) * inv

    def add_sum(row, at, value):
        lanes = slice(at, at + value.shape[1])
        sums[row, :, lanes] += jnp.sum(value.reshape(-1, 8, value.shape[1]), axis=0)

    halves = width // BLOCK

    def norm_rows(r0):
        where = [slice(n * slots + r0, n * slots + r0 + NORM_ROWS) for n in range(halves)]
        row = halves * slots + r0 % (BLOCK * 2)
        lanes = slice(r0 // (BLOCK * 2) * PAIR, r0 // (BLOCK * 2) * PAIR + PAIR)
        return where, slice(row, row + NORM_ROWS), lanes

    def keep_norm(r0, value, inv):
        where, rows, lanes = norm_rows(r0)
        for n in range(halves):
            bias[where[n], :] = value[:, n * BLOCK : (n + 1) * BLOCK]
        bias[rows, lanes] = jnp.broadcast_to(inv, (NORM_ROWS, PAIR))

    def kept_norm(r0):
        return jnp.concatenate([bias[rows, :] for rows in norm_rows(r0)[0]], axis=1)

    def kept_factor(r0):
        _, rows, lanes = norm_rows(r0)
        return bias[rows, lanes][:, :1]

    def hold(buf, value):
        for n in range(halves):
            s_scr[buf, n] = value[:, n * BLOCK : (n + 1) * BLOCK]

    def held(buf, r):
        return jnp.concatenate([s_scr[buf, n, r : r + NORM_ROWS, :] for n in range(halves)], axis=1)

    def in_turn(first, second, table):
        for i in range(nblk + 1):
            parts = []
            if i < nblk:
                parts.append(first(i))
            if i:
                parts.append(second(i - 1))
            interleave(parts)
            if table and i:
                steps(table[i - 1][0])

    def attended_rows(i):
        rows = slice(i * BLOCK, (i + 1) * BLOCK)
        at_tile = att_t[:, :, rows].reshape(width, BLOCK).T
        hold(i % 2, mm(at_tile, w_out()))
        yield

    def first_norm_rows(i):
        for r in range(0, BLOCK, NORM_ROWS):
            r0 = i * BLOCK + r
            rows = slice(r0, r0 + NORM_ROWS)
            branch_a = held(i % 2, r)
            n1, inv1 = norm(x_ref[rows, :].astype(F32) + branch_a)
            keep_norm(r0, n1, inv1)
            x_low[rows, :] = (n1 * gain_one + bias_one).astype(BF16)
            y_buf[rows, :] += branch_a
            yield

    in_turn(attended_rows, first_norm_rows, NORM_STEPS)
    steps(AFTER_NORM)

    def up_rows(i, carry):
        rows = pl.ds(aligned(i * BLOCK, BLOCK), BLOCK)
        xl = x_low[rows, :]
        for j in range(per):
            cols = slice(j * CHUNK, (j + 1) * CHUNK)
            u = mm(xl, w_up(j)) + params[4:5, cols]
            u2 = u * u
            t = jnp.tanh(u * (GELU_C + (GELU_C * GELU_K) * u2))
            h = 0.5 + 0.5 * t
            hidden[rows, cols] = (u * h).astype(BF16)
            slope = h + h * (1.0 - h) * (u * (2.0 * GELU_C + (6.0 * GELU_C * GELU_K) * u2))
            du_ref[rows, cols] = slope.astype(BF16)
        steps_in_loop(i, UP_STEPS, 0)
        return carry

    repeat(nblk, up_rows, False)
    steps(AFTER_UP)

    def down_rows(i):
        rows = slice(i * BLOCK, (i + 1) * BLOCK)
        out = None
        for j in range(per):
            part = mm(hidden[rows, j * CHUNK : (j + 1) * CHUNK], w_down(j))
            out = part if out is None else out + part
            yield
        hold(i % 2, out)

    def live_rows(r0):
        return (lax.broadcasted_iota(jnp.int32, (NORM_ROWS, width), 0) + r0) < total

    def second_norm_rows(i):
        for r in range(0, BLOCK, NORM_ROWS):
            r0 = i * BLOCK + r
            rows = slice(r0, r0 + NORM_ROWS)
            branch_f = held(i % 2, r)
            n2, inv2 = norm(kept_norm(r0) * gain_one + bias_one + branch_f)
            live = live_rows(r0)
            gx = jnp.where(live, gx_buf[rows, :].astype(F32), 0.0)
            gy = jnp.where(live, gy_buf[rows, :].astype(F32), 0.0)
            gx_buf[rows, :] = jnp.where(live, n2 * gain_two + bias_two, 0.0).astype(BF16)
            y_buf[rows, :] = jnp.where(live, y_buf[rows, :] + branch_f, 0.0)
            add_sum(3, 0, gx)
            add_sum(2, 0, gx * n2)
            dr2 = norm_back(gx, gain_two, n2, inv2)
            dx_ref[rows, :] = dr2
            df_ref[rows, :] = (dr2 + gy).astype(BF16)
            yield

    in_turn(down_rows, second_norm_rows, None)

    for j in range(per):
        part = mm_tn(hidden[:, j * CHUNK : (j + 1) * CHUNK], df_ref[...]).astype(BF16)
        part = part.reshape(-1, per, ROWS, width)
        for n in range(per):
            grads[pairs + per + n, j] = part[:, n].reshape(GRID[1:] + (ROWS, width))
    steps(AFTER_DOWN)

    def backward_rows(i, carry):
        r0 = aligned(i * BLOCK, BLOCK)
        rows = pl.ds(r0, BLOCK)
        df = df_ref[rows, :]
        dx_mid = dx_ref[rows, :]
        for j in range(per):
            cols = slice(j * CHUNK, (j + 1) * CHUNK)
            du = (mm_nt(df, w_down(j)) * du_ref[rows, cols].astype(F32)).astype(BF16)
            du_ref[rows, cols] = du
            add_sum(4, j * CHUNK, du.astype(F32))
            dx_mid = dx_mid + mm_nt(du, w_up(j))
            if j % 2:
                steps_in_loop(i, BACK_STEPS, j // 2)
        hold(i % 2, dx_mid)
        for r in range(0, BLOCK, NORM_ROWS):
            r1 = r0 + r
            own = slice(r1, r1 + NORM_ROWS)
            grad = held(i % 2, r)
            n1 = kept_norm(r1)
            gy = jnp.where(live_rows(r1), gy_buf[own, :].astype(F32), 0.0)
            add_sum(1, 0, grad)
            add_sum(0, 0, grad * n1)
            dr1 = norm_back(grad, gain_one, n1, kept_factor(r1))
            dx_ref[own, :] = dr1
            gy_buf[own, :] = (dr1 + gy).astype(BF16)
        datt_t[:, :, rows] = mm_nt(w_out(), gy_buf[rows, :]).astype(BF16).reshape(pairs, PAIR, BLOCK)
        steps_in_loop(i, BACK_STEPS, 2)
        return carry

    repeat(nblk, backward_rows, True)

    def put(p, at, value):
        grads[p, ..., at : at + value.shape[1]] = value.astype(BF16).reshape(
            GRID + (ROWS, value.shape[1])
        )

    for j in range(per):
        put(pairs + j, 0, mm_tn(x_low[...], du_ref[:, j * CHUNK : (j + 1) * CHUNK]))
        steps(UP_SUM_STEPS[j])
    part = mm(att_t[...].reshape(width, slots), gy_buf[...])
    for g in range(pairs):
        put(g, 3 * PAIR, part[:, g * PAIR : (g + 1) * PAIR])

    def gathered(n, lanes, at, r):
        row = jnp.sum(sums[n, :, lanes], axis=0, keepdims=True)
        value = jnp.broadcast_to(row, (row.shape[1] * ROWS // r, width))
        own = lax.broadcasted_iota(jnp.int32, value.shape, 0) // ROWS
        mine = own == lax.broadcasted_iota(jnp.int32, value.shape, 1) // r
        column = lax.broadcasted_iota(jnp.int32, (width, PAIR), 0)
        pick = (lax.broadcasted_iota(jnp.int32, (width, PAIR), 1) == at + column % r).astype(BF16)
        return mm(jnp.where(mine, value, 0.0).astype(BF16), pick)

    rest = [
        gathered(4, slice(j * CHUNK, (j + 1) * CHUNK), 4 * ROWS, ff * ROWS // width)
        for j in range(per)
    ]
    rest = jnp.concatenate(rest, axis=0)
    for n in range(4):
        rest = rest + gathered(n, slice(0, width), n * ROWS, ROWS)
    g_small[0] = rest.astype(BF16).reshape(GRID + (ROWS, PAIR))

    steps(OUT_SUM_STEPS)

    def ds_at(a, kb, qb=None):
        at = (0, nblk, 0, nblk - 2)[kb] * BLOCK
        lanes = slice(at, at + (nblk - kb) * BLOCK)
        if qb is not None:
            lanes = slice(at + (qb - kb) * BLOCK, at + (qb - kb + 1) * BLOCK)
        row = (2 * a + kb // 2) * BLOCK
        return slice(row, row + BLOCK), lanes

    def grads_of(g):
        return pl.ds(aligned(g * 3 * PAIR, PAIR), 3 * PAIR)

    def own_lanes(n, a):
        at = 3 * width + (2 * n + a) * PAIR
        return slice(at, at + PAIR)

    lane = lax.broadcasted_iota(jnp.int32, (slots, PAIR), 1)

    def put_halves(n, value):
        value = value.astype(F32)
        du_ref[:, own_lanes(n, 0)] = jnp.where(lane < HALF, value, 0.0).astype(BF16)
        du_ref[:, own_lanes(n, 1)] = jnp.where(lane < HALF, 0.0, value).astype(BF16)

    turned = slice(slots, 2 * slots)
    key_rows, do_rows = BLOCK, BLOCK + PAIR

    def attend_back(g, carry):
        def put_grad(n, block, value):
            rows = slice(block * BLOCK, (block + 1) * BLOCK)
            lanes = pl.ds(aligned(g * 3 * PAIR + n * PAIR, PAIR), PAIR)
            du_ref[rows, lanes] = value.astype(BF16)

        hidden[key_rows : key_rows + PAIR, turned] = kv_ref[g, :, :PAIR].T
        for a in range(2):
            heads = slice(a * HALF, (a + 1) * HALF)
            scaled = datt_t[g, heads, :].astype(F32) * inverses[2 * g + a]
            dots = jnp.sum(att_t[g, heads, :].astype(F32) * scaled, axis=0, keepdims=True)
            inverses[2 * g + a] = dots
            hidden[do_rows + a * HALF : do_rows + (a + 1) * HALF, turned] = scaled.astype(BF16)
        put_halves(0, hidden[do_rows : do_rows + PAIR, turned].T)
        put_halves(1, q_t[g].T)
        steps_in_loop(g, ATTEND_BACK_STEPS, 0)

        def through_values(unit, buf):
            qb, a = unit
            nk = (qb + 1) * BLOCK
            do = half_rows(hidden[do_rows : do_rows + PAIR, slots + qb * BLOCK : slots + nk], a)
            s_scr[buf, : qb + 1] = mm(kv_ref[g, :nk, PAIR:], do).reshape(qb + 1, BLOCK, BLOCK)
            yield

        def through_softmax(unit, buf):
            qb, a = unit
            dots = inverses[2 * g + a, :, qb * BLOCK : (qb + 1) * BLOCK]
            for r in range(0, (qb + 1) * BLOCK, SPAN):
                inner = slice(r % BLOCK, r % BLOCK + SPAN)
                p = probs[2 * g + a, inner, across(r // BLOCK, qb)].astype(F32)
                rows, lanes = ds_at(a, r // BLOCK, qb)
                ds = p * (s_scr[buf, r // BLOCK, inner] - dots)
                hidden[rows.start + r % BLOCK : rows.start + r % BLOCK + SPAN, lanes] = ds.astype(BF16)
                yield

        def to_queries(unit, kept):
            qb, a = unit
            out = None
            for kb in range(qb + 1):
                keys = slice(slots + kb * BLOCK, slots + (kb + 1) * BLOCK)
                k = hidden[key_rows + a * HALF : key_rows + (a + 1) * HALF, keys]
                part = mm(k, hidden[ds_at(a, kb, qb)])
                out = part if out is None else out + part
                yield
            kept[unit] = out * (HALF**-0.5)
            if a:
                put_grad(0, qb, jnp.concatenate([kept[qb, 0], kept[qb, 1]], axis=0).T)

        def to_values(unit, kept):
            kb, a = unit
            kept[unit] = mm(probs[2 * g + a, :, seen_by(kb)], du_ref[kb * BLOCK :, own_lanes(0, a)])
            yield
            if a:
                put_grad(2, kb, kept[kb, 0] + kept[kb, 1])

        def to_keys(unit, kept):
            kb, a = unit
            kept[unit] = mm(hidden[ds_at(a, kb)], du_ref[kb * BLOCK :, own_lanes(1, a)])
            yield
            if a:
                put_grad(1, kb, kept[kb, 0] + kept[kb, 1])

        kept = {}, {}, {}
        units = [(qb, a) for qb in reversed(range(nblk)) for a in range(2)]
        for t in range(len(units) + 2):
            parts = []
            if t < len(units):
                parts.append(through_values(units[t], t % 2))
                parts.append(to_values(units[t], kept[0]))
            if 1 <= t <= len(units):
                parts.append(through_softmax(units[t - 1], (t - 1) % 2))
            if t >= 2:
                parts.append(to_queries(units[t - 2], kept[1]))
                parts.append(to_keys(units[t - 2], kept[2]))
            interleave(parts)
            if t % 2 and t > 1:
                steps_in_loop(g, ATTEND_BACK_STEPS, t // 2)
        put(g, 0, mm(x_t[...], du_ref[:, grads_of(g)]))
        steps_in_loop(g, ATTEND_BACK_STEPS, 1 + nblk)
        return carry

    repeat(pairs, attend_back, True)

    for qb in range(nblk):
        rows = slice(qb * BLOCK, (qb + 1) * BLOCK)
        total_dx = dx_ref[rows, :]
        for g in range(pairs):
            grad = du_ref[rows, g * 3 * PAIR : (g + 1) * 3 * PAIR]
            total_dx = total_dx + mm_nt(grad, w_qkv(g))
        dx_ref[rows, :] = total_dx
        steps(INPUT_STEPS[qb])
    steps(LAST_STEPS)
    if linked:
        gather_small.step(5, 0)
        scatter_small.step(5, 0)
        for p in range(PIECES):
            gather.step(5, p)
            scatter.step(5, p)


def layer(linked, x_in, y_in, lengths, grad_x, grad_y, *rest):
    slots, width = x_in.shape
    ff = 4 * width
    nblk = slots // BLOCK
    pairs = H // 2
    causal = BLOCK * nblk * (nblk + 1) // 2
    vmem = pl.BlockSpec(memory_space=pltpu.VMEM)
    any_ = pl.BlockSpec(memory_space=pl.ANY)
    smem = pl.BlockSpec(memory_space=pltpu.SMEM)
    streams = tuple(pltpu.VMEM((slots, width), dtype) for dtype in (BF16, F32, F32))
    wide = (PIECES,) + GRID + (ROWS, CHUNK)
    narrow = (1,) + GRID + (ROWS, PAIR)
    links = []
    if linked:
        outs = [
            pltpu.VMEM((PIECES, ROWS, CHUNK), F32),
            pltpu.VMEM((ROWS, PAIR), F32),
        ]
        links += [pltpu.VMEM(wide, BF16), pltpu.VMEM(wide, BF16)]
        links += [pltpu.VMEM(narrow, BF16), pltpu.VMEM(narrow, BF16)]
        for n, _, _, _, _, r, lanes in (wide, narrow):
            links += [
                pltpu.VMEM((n, 4, 2, 2, r, lanes), BF16),
                pltpu.VMEM((n, 2, 2, 2, r, lanes), BF16),
                pltpu.VMEM((n, 2, 2, r, lanes), BF16),
                pltpu.VMEM((n, 3, r, lanes), BF16),
                pltpu.VMEM((3, 4, r, lanes), BF16),
            ]
        for n in (PIECES, 1, PIECES, 1):
            links += [pltpu.SemaphoreType.DMA((n, Z + 4)), pltpu.SemaphoreType.DMA((n, Z + 4))]
        params = pltpu.CompilerParams(
            vmem_limit_bytes=VMEM_LIMIT, collective_id=0, has_side_effects=True
        )
    else:
        outs = [jax.ShapeDtypeStruct(wide, BF16), jax.ShapeDtypeStruct(narrow, BF16)]
        params = pltpu.CompilerParams(vmem_limit_bytes=VMEM_LIMIT)
    return pl.pallas_call(
        functools.partial(layer_kernel, linked),
        out_shape=streams + tuple(outs),
        in_specs=[smem] + [any_] * 4 + [vmem] * len(rest),
        out_specs=(vmem,) * (3 + len(outs)),
        scratch_shapes=links
        + [
            pltpu.VMEM((slots, width), BF16),
            pltpu.VMEM((slots, width), BF16),
            pltpu.VMEM((8, ff), F32),
            pltpu.VMEM((5, 8, ff), F32),
            pltpu.VMEM((pairs, slots, 2 * PAIR), BF16),
            pltpu.VMEM((pairs, PAIR, slots), BF16),
            pltpu.VMEM((pairs, PAIR, slots), BF16),
            pltpu.VMEM((H, 1, slots), F32),
            pltpu.VMEM((pairs, PAIR, slots), BF16),
            pltpu.VMEM((H, BLOCK, causal), BF16),
            pltpu.VMEM((causal, BLOCK), F32),
            pltpu.VMEM((slots, ff), BF16),
            pltpu.VMEM((slots, ff), BF16),
            pltpu.VMEM((slots, width), BF16),
            pltpu.VMEM((slots, width), BF16),
            pltpu.VMEM((width, slots), BF16),
            pltpu.VMEM((2, nblk, BLOCK, BLOCK), F32),
            pltpu.SemaphoreType.DMA((4,)),
        ],
        compiler_params=params,
        name="layer",
    )(lengths, x_in, y_in, grad_x, grad_y, *rest)


def deliver_kernel(x_out, y_out, d_x, shares, small, *refs):
    streams, (d_qkv, d_out, d_up, d_down), vectors, sem = refs[:3], refs[3:7], refs[7:12], refs[12]
    copies = [
        pltpu.make_async_copy(src, dst, sem.at[n])
        for n, (src, dst) in enumerate(zip((x_out, y_out, d_x), streams))
    ]
    for cp in copies:
        cp.start()
    pairs, width = H // 2, d_out.shape[1]
    for g in range(pairs):
        for n in range(3):
            lanes = slice(n * width + g * PAIR, n * width + (g + 1) * PAIR)
            d_qkv[:, lanes] = shares[g, :, n * PAIR : (n + 1) * PAIR]
        d_out[:, g * PAIR : (g + 1) * PAIR] = shares[g, :, 3 * PAIR :]
    per = d_up.shape[1] // CHUNK
    for j in range(per):
        d_up[:, j * CHUNK : (j + 1) * CHUNK] = shares[pairs + j]
        d_down[j * ROWS : (j + 1) * ROWS, :] = shares[pairs + per + j]
    at = 0
    for ref in vectors:
        ref[...] = small[0, at : at + ref.shape[0]]
        at += ref.shape[0]
    for cp in copies:
        cp.wait()


def deliver(streams, shares, small, shapes):
    vmem = pl.BlockSpec(memory_space=pltpu.VMEM)
    any_ = pl.BlockSpec(memory_space=pl.ANY)
    outs = [jax.ShapeDtypeStruct(s.shape, s.dtype) for s in streams]
    outs += [jax.ShapeDtypeStruct(shape, F32) for shape in shapes]
    return pl.pallas_call(
        deliver_kernel,
        out_shape=outs,
        in_specs=[vmem] * 5,
        out_specs=[any_] * 3 + [vmem] * 9,
        scratch_shapes=[pltpu.SemaphoreType.DMA((3,))],
        compiler_params=pltpu.CompilerParams(vmem_limit_bytes=DELIVER_LIMIT),
        name="deliver",
    )(*(pltpu.with_memory_space_constraint(v, pltpu.VMEM) for v in (*streams, shares, small)))


BOTH = ("dp", "fsdp")


def on_device(
    linked,
    x_in,
    y_in,
    lengths,
    w_qkv,
    w_out,
    gain_one,
    bias_one,
    w_up,
    b_up,
    w_down,
    gain_two,
    bias_two,
    grad_x,
    grad_y,
):
    streams = (x_in, y_in, lengths, grad_x, grad_y)
    width = x_in.shape[1]
    if linked:
        ends = (gain_one, bias_one, gain_two, bias_two, b_up)
        *out_streams, shares, small = layer(True, *streams, w_qkv, w_out, w_up, w_down, *ends)
        shapes = [w.shape for w in (w_qkv, w_out, w_up, w_down) + ends]
        x_out, y_out, d_x, d_qkv, d_out, d_up, d_down, *vectors = deliver(
            out_streams, shares, small, shapes
        )
    else:
        blocks = GRID[0] * GRID[1] * GRID[2] * GRID[3]
        pairs = H // 2

        def whole(w):
            return lax.all_gather(w, BOTH, axis=0, tiled=True)

        def cut(w):
            return w.reshape(GRID + (ROWS, CHUNK))

        qkv, out, up, down = (whole(w) for w in (w_qkv, w_out, w_up, w_down))
        pieces = []
        for g in range(pairs):
            lane = [slice(n * width + g * PAIR, n * width + (g + 1) * PAIR) for n in range(3)]
            pieces.append(cut(jnp.concatenate([qkv[:, s] for s in lane] + [out[:, lane[0]]], 1)))
        per = up.shape[1] // CHUNK
        pieces += [cut(up[:, j * CHUNK : (j + 1) * CHUNK]) for j in range(per)]
        down = down.reshape(blocks, per, ROWS, width)
        pieces += [cut(down[:, j].reshape(-1, width)) for j in range(per)]
        vectors = [whole(v) for v in (gain_one, bias_one, gain_two, bias_two, b_up)]
        small = jnp.concatenate([v.reshape(blocks, -1) for v in vectors], axis=1)
        small = jnp.broadcast_to(small[:, None], (blocks, ROWS, small.shape[1]))
        x_out, y_out, d_x, grads, d_small = layer(
            False, *streams, jnp.stack(pieces), small.reshape((1,) + GRID + (ROWS, -1))
        )

        def share(w):
            return lax.psum_scatter(w, BOTH, scatter_dimension=0, tiled=True)

        grads = grads.astype(F32).reshape(PIECES, -1, CHUNK)
        d_qkv = grads[:pairs, :, : 3 * PAIR].reshape(pairs, width, 3, PAIR)
        d_qkv = share(d_qkv.transpose(1, 2, 0, 3).reshape(width, 3 * width))
        d_out = share(grads[:pairs, :, 3 * PAIR :].transpose(1, 0, 2).reshape(width, width))
        d_up = share(grads[pairs : pairs + per].transpose(1, 0, 2).reshape(width, -1))
        d_down = grads[pairs + per :].reshape(per, blocks, ROWS, width).transpose(1, 0, 2, 3)
        d_down = share(d_down.reshape(-1, width))
        rows = d_small.astype(F32).reshape(blocks, ROWS, -1)[:, 0]
        vectors = [share(rows[:, n * ROWS : (n + 1) * ROWS].reshape(-1)) for n in range(4)]
        vectors.append(share(rows[:, 4 * ROWS :].reshape(-1)))
    return (
        x_out,
        y_out,
        d_x,
        d_qkv,
        d_out,
        vectors[0],
        vectors[1],
        d_up,
        vectors[4],
        d_down,
        vectors[2],
        vectors[3],
    )


def solution(mesh):
    matrix, vector = P(BOTH, None), P(BOTH)
    linked = mesh.shape["dp"] == Z and mesh.shape["fsdp"] == GRID[1] * GRID[2] * GRID[3]
    return jax.shard_map(
        functools.partial(on_device, linked),
        mesh=mesh,
        in_specs=(matrix,) * 5
        + (vector, vector, matrix, vector, matrix, vector, vector, matrix, matrix),
        out_specs=(matrix,) * 5
        + (vector, vector, matrix, vector, matrix, vector, vector),
        check_vma=False,
    )
```

```python
import functools

import jax
import jax.numpy as jnp
from jax import lax
from jax.experimental import pallas as pl
from jax.experimental.pallas import tpu as pltpu
from jax.sharding import PartitionSpec as P

H = 8
PAIR = 128
HALF = 64
BLOCK = 256
CHUNK = 512
SPAN = 128
GRID = (4, 2, 2, 2)
ROWS = 16
Z = GRID[0]
PIECES = 12
NORM_ROWS = 64
FIRST_PIECE = 0
LAST_PIECE = 3
VMEM_LIMIT = 67000000
EPSILON = 1e-05
NEGATIVE = -1e30
GELU_C = 0.7978845608028654
GELU_K = 0.044715
F32 = jnp.float32
BF16 = jnp.bfloat16
MESH = pl.DeviceIdType.MESH


def mm(a, b):
    return lax.dot_general(a, b, (((1,), (0,)), ((), ())), preferred_element_type=F32)


def mm_nt(a, b):
    return lax.dot_general(a, b, (((1,), (1,)), ((), ())), preferred_element_type=F32)


def mm_tn(a, b):
    return lax.dot_general(a, b, (((0,), (0,)), ((), ())), preferred_element_type=F32)


def interleave(parts):
    while parts:
        for part in list(parts):
            try:
                next(part)
            except StopIteration:
                parts.remove(part)


def aligned(value, n):
    return value if isinstance(value, int) else pl.multiple_of(value, n)


def repeat(n, body, unrolled):
    if unrolled:
        for i in range(n):
            body(i, 0)
    else:
        lax.fori_loop(0, n, body, 0)


class Place:
    def __init__(self):
        self.z = lax.axis_index("dp")
        inner = lax.axis_index("fsdp")
        self.c = lax.rem(inner, 2)
        self.x = lax.rem(inner // 2, 2)
        self.y = inner // 4

    def device(self, z, y, x, c):
        return (z, (y * 2 + x) * 2 + c)

    def around(self, d):
        return lax.rem(self.z + d, Z)


LOW, HIGH, EVERY = slice(0, Z // 2), slice(Z // 2, Z), slice(None)


class Gather:
    def __init__(self, place, buf, send, recv, straight=()):
        self.at, self.buf, self.send, self.recv, self.straight = place, buf, send, recv, straight

    def copy(self, block, target, p, n):
        ref = self.buf.at[block]
        return pltpu.make_async_remote_copy(
            src_ref=ref,
            dst_ref=ref,
            send_sem=self.send.at[p, n],
            recv_sem=self.recv.at[p, n],
            device_id=target,
            device_id_type=MESH,
        )

    def along_z(self, p, d, source):
        a = self.at
        return self.copy((p, source, a.y, a.x, a.c), a.device(a.around(d), a.y, a.x, a.c), p, d - 1)

    def plane(self, p, n, zs, y, x, along):
        a = self.at
        ty = a.y if along == "x" else 1 - a.y
        tx = a.x if along == "y" else 1 - a.x
        return self.copy((p, zs, y, x, a.c), a.device(a.z, ty, tx, a.c), p, Z - 1 + n)

    def core(self, p, c):
        a = self.at
        return self.copy((p, EVERY, EVERY, EVERY, c), a.device(a.z, a.y, a.x, 1 - a.c), p, Z + 3)

    def step(self, n, p):
        a = self.at
        y, x = a.y, a.x
        once = isinstance(p, int) and p in self.straight
        if n == 0:
            for d in range(1, Z):
                self.along_z(p, d, a.z).start()
        elif n == 1:
            for d in range(1, Z):
                self.along_z(p, d, a.around(Z - d)).wait_recv()
            if once:
                self.plane(p, 2, EVERY, y, x, "xy").start()
            self.plane(p, 0, EVERY, y, x, "x").start()
            self.plane(p, 1, EVERY, y, x, "y").start()
        elif n == 2 and not once:
            self.plane(p, 0, EVERY, y, 1 - x, "x").wait_recv()
            self.plane(p, 2, LOW, y, 1 - x, "y").start()
            self.plane(p, 1, EVERY, 1 - y, x, "y").wait_recv()
            self.plane(p, 3, HIGH, 1 - y, x, "x").start()
        elif n == 3:
            if once:
                self.plane(p, 0, EVERY, y, 1 - x, "x").wait_recv()
                self.plane(p, 1, EVERY, 1 - y, x, "y").wait_recv()
                self.plane(p, 2, EVERY, 1 - y, 1 - x, "xy").wait_recv()
            else:
                self.plane(p, 2, LOW, 1 - y, 1 - x, "y").wait_recv()
                self.plane(p, 3, HIGH, 1 - y, 1 - x, "x").wait_recv()
            self.core(p, a.c).start()
        elif n == 4:
            self.core(p, 1 - a.c).wait_recv()
        elif n == 5:
            for d in range(1, Z):
                self.along_z(p, d, a.z).wait_send()
            self.plane(p, 0, EVERY, y, x, "x").wait_send()
            self.plane(p, 1, EVERY, y, x, "y").wait_send()
            if once:
                self.plane(p, 2, EVERY, y, x, "xy").wait_send()
            else:
                self.plane(p, 2, LOW, y, 1 - x, "y").wait_send()
                self.plane(p, 3, HIGH, 1 - y, x, "x").wait_send()
            self.core(p, a.c).wait_send()


class Scatter:
    def __init__(self, place, buf, got_core, got_first, got_second, got_z, got_last, send, recv, finish, straight=()):
        self.at, self.buf, self.straight = place, buf, straight
        self.got_core, self.got_first = got_core, got_first
        self.got_second, self.got_z, self.got_last = got_second, got_z, got_last
        self.send, self.recv, self.finish = send, recv, finish

    def copy(self, src, dst, target, p, n):
        return pltpu.make_async_remote_copy(
            src_ref=src,
            dst_ref=dst,
            send_sem=self.send.at[p, n],
            recv_sem=self.recv.at[p, n],
            device_id=target,
            device_id_type=MESH,
        )

    def core(self, p):
        a = self.at
        src = self.buf.at[p, EVERY, EVERY, EVERY, 1 - a.c]
        return self.copy(src, self.got_core.at[p], a.device(a.z, a.y, a.x, 1 - a.c), p, 0)

    def plane(self, p, n):
        a = self.at
        along_x, along_y = a.device(a.z, a.y, 1 - a.x, a.c), a.device(a.z, 1 - a.y, a.x, a.c)
        if n == 1:
            return self.copy(self.buf.at[p, LOW, :, 1 - a.x, a.c], self.got_first.at[p, 0], along_x, p, n)
        if n == 2:
            return self.copy(self.buf.at[p, HIGH, 1 - a.y, :, a.c], self.got_first.at[p, 1], along_y, p, n)
        if n == 3:
            return self.copy(self.buf.at[p, LOW, 1 - a.y, a.x, a.c], self.got_second.at[p, 0], along_y, p, n)
        return self.copy(self.buf.at[p, HIGH, a.y, 1 - a.x, a.c], self.got_second.at[p, 1], along_x, p, n)

    def at_once(self, p, n):
        a = self.at
        y = a.y if n == 1 else 1 - a.y
        x = a.x if n == 2 else 1 - a.x
        target = a.device(a.z, y, x, a.c)
        return self.copy(self.buf.at[p, :, y, x, a.c], self.got_last.at[n - 1], target, p, n)

    def along_z(self, p, d):
        a = self.at
        z = a.around(d)
        target = a.device(z, a.y, a.x, a.c)
        return self.copy(self.buf.at[p, z, a.y, a.x, a.c], self.got_z.at[p, d - 1], target, p, 4 + d)

    def add(self, block, *values):
        total = self.buf[block].astype(F32)
        for value in values:
            total = total + value.astype(F32)
        self.buf[block] = total.astype(BF16)

    def step(self, n, p):
        a = self.at
        once = isinstance(p, int) and p in self.straight
        if n == 0:
            self.core(p).start()
        elif n == 1:
            self.core(p).wait_recv()
            self.add((p, EVERY, EVERY, EVERY, a.c), self.got_core[p])
            for k in (3, 1, 2) if once else (1, 2):
                (self.at_once(p, k) if once else self.plane(p, k)).start()
        elif n == 2 and not once:
            self.plane(p, 1).wait_recv()
            self.add((p, LOW, EVERY, a.x, a.c), self.got_first[p, 0])
            self.plane(p, 3).start()
            self.plane(p, 2).wait_recv()
            self.add((p, HIGH, a.y, EVERY, a.c), self.got_first[p, 1])
            self.plane(p, 4).start()
        elif n == 3:
            own = (p, EVERY, a.y, a.x, a.c)
            if once:
                for k in (1, 2, 3):
                    self.at_once(p, k).wait_recv()
                self.add(own, self.got_last[0], self.got_last[1], self.got_last[2])
            else:
                for k in (3, 4):
                    self.plane(p, k).wait_recv()
                self.add(own, as_matrix(self.got_second[p]).reshape(Z, ROWS, -1))
            for d in range(1, Z):
                self.along_z(p, d).start()
        elif n == 4:
            total = self.buf[p, a.z, a.y, a.x, a.c].astype(F32)
            for d in range(1, Z):
                self.along_z(p, d).wait_recv()
                total = total + self.got_z[p, d - 1].astype(F32)
            self.finish(p, total)
        elif n == 5:
            self.core(p).wait_send()
            for k in (1, 2, 3) if once else (1, 2, 3, 4):
                (self.at_once(p, k) if once else self.plane(p, k)).wait_send()
            for d in range(1, Z):
                self.along_z(p, d).wait_send()


SMALL = "small"
START_STEPS = (
    ((False, 0, 0), (False, 0, 1), (False, 0, 2), (False, 0, 3), (False, SMALL, 0),),
    (),
    (),
    (),
    (),
    ((False, 1, 0), (False, 2, 0), (False, 0, 4), (False, 1, 1), (False, 0, 5), (False, 1, 2), (False, 0, 6), (False, 1, 3), (False, 0, 7), (False, 3, 0),),
)
ATTEND_STEPS = (
    (((False, 1, 4), (False, 0, 8), (False, 4, 0), (False, 2, 1),), ((False, 1, 5), (False, 0, 9),), ((False, 2, 2), (False, SMALL, 1),), ((False, 1, 6), (False, 0, 10),), (), ((False, 2, 3),),),
    (((False, 2, 4), (False, 3, 1), (False, 1, 7), (False, 0, 11), (False, 4, 1), (False, 2, 5),), ((False, 3, 2), (False, 1, 8),), ((False, SMALL, 2),), (), ((False, 4, 2), (False, 2, 6),), ((False, 3, 3), (False, 1, 9),),),
    ((), ((False, 3, 4), (False, 1, 10),), ((False, 4, 3), (False, SMALL, 3),), ((False, 2, 7),), ((False, 4, 4), (False, 3, 5), (False, 1, 11),), (),),
    ((), ((False, 4, 5), (False, 2, 8), (False, 3, 6),), (), (), ((False, 4, 6), (False, 2, 9),), (),),
)
AFTER_ATTEND = ((False, SMALL, 4),)
NORM_STEPS = (
    (((False, 2, 10),),),
    (((False, 3, 7),),),
    ((),),
    (((False, 4, 7), (False, 2, 11),),),
)
AFTER_NORM = ()
UP_STEPS = (
    (((False, 3, 8), (False, 3, 9),),),
    (((False, 3, 10),),),
    (((False, 4, 8), (False, 4, 9), (False, 3, 11), (False, 4, 10),),),
    ((),),
)
AFTER_UP = ((False, 4, 11),)
AFTER_DOWN = ((True, 0, 0), (True, 0, 1), (True, 0, 2), (True, 0, 3),)
BACK_STEPS = (
    ((), (), ((True, 1, 0),),),
    (((True, 1, 1), (True, 1, 2),), ((True, 1, 3),), (),),
    ((), (), ((True, 2, 0),),),
    ((), ((True, 2, 1),), ((True, 2, 2),),),
)
UP_SUM_STEPS = (
    ((True, 0, 4),),
    ((True, 2, 3), (True, 3, 0), (True, 0, 5),),
    ((True, 0, 6),),
    ((True, 3, 1), (True, 1, 4), (True, 0, 7),),
)
OUT_SUM_STEPS = ((True, SMALL, 0), (True, 3, 2), (True, 1, 5), (True, 1, 6),)
ATTEND_BACK_STEPS = (
    (((True, 3, 3),), ((True, 4, 0), (True, 1, 7),), ((True, 2, 4), (True, 4, 1),), ((True, SMALL, 1),), ((True, 2, 5), (True, 4, 2),), ((True, 0, 8),),),
    (((True, 2, 6),), ((True, 4, 3), (True, 2, 7),), ((True, 3, 4), (True, 3, 5), (True, 1, 8),), ((True, SMALL, 2),), ((True, 3, 6),), ((True, 0, 9),),),
    ((), ((True, 3, 7),), ((True, 4, 4), (True, 2, 8), (True, 1, 9),), ((True, SMALL, 3),), ((True, 4, 5),), ((True, 0, 10),),),
    (((True, 4, 6),), ((True, 4, 7), (True, 3, 8),), ((True, 1, 10), (True, 2, 9),), ((True, SMALL, 4),), (), ((True, 0, 11),),),
)
INPUT_STEPS = (
    ((True, 4, 8),),
    ((True, 2, 10), (True, 1, 11), (True, 3, 9),),
    ((True, 2, 11),),
    (),
)
LAST_STEPS = ((True, 3, 10), (True, 4, 9), (True, 3, 11), (True, 4, 10), (True, 4, 11),)


def piece_at(order):
    if isinstance(order, int):
        return (8, 4, 0)[order // 4] + order % 4
    return jnp.where(order < 4, order + 8, jnp.where(order < 8, order, order - 8))


def as_matrix(value):
    return value.reshape(-1, value.shape[-1])


def layer_kernel(linked, *refs):
    refs = list(refs)

    def take(n):
        out = refs[:n]
        del refs[:n]
        return out

    lengths_ref, x_hbm, y_hbm, gx_hbm, gy_hbm = take(5)
    if linked:
        s_qkv, s_out, s_up, s_down = take(4)
        vectors = take(5)
        xo_hbm, yo_hbm, dx_hbm, shares, o_small = take(5)
        weights, grads, small, g_small = take(4)
        got = take(10)
        sems = take(8)
    else:
        weights, small = take(2)
        xo_hbm, yo_hbm, dx_hbm, grads, g_small = take(5)
    (
        x_ref,
        gx_buf,
        y_buf,
        dx_ref,
        gy_buf,
        params,
        sums,
        kv_ref,
        q_t,
        att_t,
        inverses,
        datt_t,
        probs,
        bias,
        hidden,
        du_ref,
        x_low,
        df_ref,
        x_t,
        s_scr,
        in_sem,
        out_sem,
    ) = refs

    slots, width = x_ref.shape
    nblk = slots // BLOCK
    ff = hidden.shape[1]
    pairs = H // 2
    per = ff // CHUNK

    loads = []
    for n, (src, dst) in enumerate(
        ((x_hbm, x_ref), (y_hbm, y_buf), (gx_hbm, gx_buf), (gy_hbm, gy_buf))
    ):
        cp = pltpu.make_async_copy(src, dst, in_sem.at[n])
        cp.start()
        loads.append(cp)

    if linked:
        place = Place()
        z, y, x, c = place.z, place.y, place.x, place.c
        barrier = pltpu.get_barrier_semaphore()
        partners = [
            place.device(z, y, x, 1 - c),
            place.device(z, y, 1 - x, c),
            place.device(z, 1 - y, x, c),
            place.device(z, 1 - y, 1 - x, c),
        ] + [place.device(place.around(d), y, x, c) for d in range(1, Z)]
        for partner in partners:
            pl.semaphore_signal(barrier, inc=1, device_id=partner, device_id_type=MESH)
        for g in range(pairs):
            lanes = [slice(n * width + g * PAIR, n * width + (g + 1) * PAIR) for n in range(3)]
            own = [s_qkv[:, lane] for lane in lanes] + [s_out[:, lanes[0]]]
            weights[g, z, y, x, c] = jnp.concatenate(own, axis=1)
        for j in range(per):
            weights[pairs + j, z, y, x, c] = s_up[:, j * CHUNK : (j + 1) * CHUNK]
            weights[pairs + per + j, z, y, x, c] = s_down[j * ROWS : (j + 1) * ROWS, :]
        packed = jnp.zeros((ROWS, PAIR), F32)
        at = 0
        for ref in vectors:
            r = ref.shape[0]
            row = jnp.broadcast_to(ref[...].astype(F32).reshape(1, r), (ROWS, r)).astype(BF16)
            column = lax.broadcasted_iota(jnp.int32, (r, PAIR), 1)
            packed += mm(row, (column == lax.broadcasted_iota(jnp.int32, (r, PAIR), 0) + at).astype(BF16))
            at += r
        small[0, z, y, x, c] = packed.astype(BF16)
        pl.semaphore_wait(barrier, len(partners))

        def finish(p, total):
            shares[p] = total

        def finish_small(p, total):
            o_small[...] = total

        gather = Gather(place, weights, sems[0], sems[1], (FIRST_PIECE,))
        gather_small = Gather(place, small, sems[2], sems[3])
        scatter = Scatter(place, grads, *got[:5], sems[4], sems[5], finish, (LAST_PIECE,))
        scatter_small = Scatter(place, g_small, *got[5:], sems[6], sems[7], finish_small)
    def run_step(scattered, n, order):
        if scattered:
            scatter.step(n, piece_at(order))
        else:
            gather.step(n, order)

    def steps(events):
        if linked:
            for event in events:
                if event[1] == SMALL:
                    (scatter_small if event[0] else gather_small).step(event[2], 0)
                else:
                    run_step(*event)

    def steps_in_loop(i, table, slot):
        if not linked:
            return
        if isinstance(i, int):
            steps(table[i][slot])
            return
        kinds = []
        for row in table:
            for event in row[slot]:
                if event[1] != SMALL and event[:2] not in kinds:
                    kinds.append(event[:2])
        kinds.sort(key=lambda kind: kind[1])
        for kind in kinds:
            columns = [[e[2] for e in row[slot] if e[:2] == kind] for row in table]
            for k in range(max(len(column) for column in columns)):
                have = [j for j, column in enumerate(columns) if len(column) > k]
                order = jnp.int32(columns[have[0]][k])
                wanted = i == have[0]
                for j in have[1:]:
                    order = jnp.where(i == j, columns[j][k], order)
                    wanted = wanted | (i == j)
                if len(have) == len(columns):
                    run_step(*kind, order)
                else:
                    pl.when(wanted)(functools.partial(run_step, *kind, order))
        for j, row in enumerate(table):
            for e in row[slot]:
                if e[1] == SMALL:
                    pl.when(i == j)(functools.partial(steps, (e,)))

    def segments(pos):
        seg = jnp.zeros(pos.shape, jnp.int32)
        end = jnp.int32(0)
        for j in range(lengths_ref.shape[1]):
            end = end + lengths_ref[0, j]
            seg = seg + (end <= pos).astype(jnp.int32)
        return jnp.where(pos < end, seg, -1 - pos), end

    starts = [BLOCK * (qb * (qb + 1) // 2) for qb in range(nblk)]
    steps(START_STEPS[0])
    for qb in range(nblk):
        q_pos = lax.broadcasted_iota(jnp.int32, (1, BLOCK), 1) + qb * BLOCK
        q_seg, total = segments(q_pos)
        for kb in range(qb + 1):
            k_pos = lax.broadcasted_iota(jnp.int32, (BLOCK, 1), 0) + kb * BLOCK
            k_seg, _ = segments(k_pos)
            allowed = k_seg == q_seg
            if kb == qb:
                allowed = allowed & (k_pos <= q_pos)
            at = starts[qb] + kb * BLOCK
            bias[at : at + BLOCK, :] = jnp.where(allowed, 0.0, NEGATIVE).astype(F32)
        steps(START_STEPS[1 + qb])

    loads[0].wait()
    x_t[...] = x_ref[...].T

    def spread(first, at, r):
        rows = first.shape[0]
        column = lax.broadcasted_iota(jnp.int32, (PAIR, width), 1)
        pick = (lax.broadcasted_iota(jnp.int32, (PAIR, width), 0) == at + column % r).astype(BF16)
        own = lax.broadcasted_iota(jnp.int32, (rows, width), 0)
        mine = own == (lax.broadcasted_iota(jnp.int32, (rows, width), 1) // r) * ROWS
        return jnp.sum(jnp.where(mine, mm(first, pick), 0.0), axis=0, keepdims=True)

    def w_qkv(g):
        return as_matrix(weights[g, ..., : 3 * PAIR])

    def w_out():
        return jnp.concatenate(
            [as_matrix(weights[g, ..., 3 * PAIR :]) for g in range(pairs)], axis=1
        )

    def w_up(j):
        return as_matrix(weights[pairs + j])

    def w_down(j):
        parts = [weights[pairs + per + n, j].reshape(-1, ROWS, width) for n in range(per)]
        return as_matrix(jnp.stack(parts, axis=1))

    steps(START_STEPS[1 + nblk])

    def across(kb, qb):
        at = BLOCK * (kb * nblk - kb * (kb - 1) // 2 + qb - kb)
        return slice(at, at + BLOCK)

    def seen_by(kb):
        return slice(across(kb, kb).start, across(kb, nblk - 1).stop)

    def half_rows(value, a):
        own = value[a * HALF : (a + 1) * HALF]
        rest = jnp.zeros_like(own)
        return jnp.concatenate([rest, own] if a else [own, rest], axis=0)

    def attend(g, carry):
        steps_in_loop(g, ATTEND_STEPS, 0)
        weights_g = w_qkv(g)
        for qb in range(nblk):
            rows = slice(qb * BLOCK, (qb + 1) * BLOCK)
            kv_ref[g, rows, :] = mm(x_ref[rows, :], weights_g[:, PAIR:]).astype(BF16)
        q = mm_tn(weights_g[:, :PAIR], x_t[...]).astype(BF16).astype(F32)
        q_t[g] = (q * (HALF**-0.5)).astype(BF16)
        v_t = kv_ref[g, :, PAIR:].T
        steps_in_loop(g, ATTEND_STEPS, 1)

        def scores(unit, buf):
            qb, a = unit
            nk = (qb + 1) * BLOCK
            part = mm(kv_ref[g, :nk, :PAIR], half_rows(q_t[g, :, qb * BLOCK : nk], a))
            s_scr[buf, : qb + 1] = part.reshape(qb + 1, BLOCK, BLOCK)
            yield

        def masked(unit, buf, r):
            at = starts[unit[0]] + r
            return s_scr[buf, r // BLOCK, r % BLOCK : r % BLOCK + SPAN] + bias[at : at + SPAN, :]

        def soften(unit, buf):
            qb, a = unit
            top = None
            for r in range(0, (qb + 1) * BLOCK, SPAN):
                high = jnp.max(masked(unit, buf, r).reshape(-1, 8, BLOCK), axis=0)
                top = high if top is None else jnp.maximum(top, high)
                yield
            top = jnp.max(top, axis=0, keepdims=True)
            whole = None
            for r in range(0, (qb + 1) * BLOCK, SPAN):
                e = jnp.exp(masked(unit, buf, r) - top)
                one = jnp.sum(e.reshape(-1, 8, BLOCK), axis=0)
                whole = one if whole is None else whole + one
                lanes = across(r // BLOCK, qb)
                probs[2 * g + a, r % BLOCK : r % BLOCK + SPAN, lanes] = e.astype(BF16)
                yield
            whole = jnp.sum(whole, axis=0, keepdims=True)
            inverses[2 * g + a, :, qb * BLOCK : (qb + 1) * BLOCK] = 1.0 / whole

        def mix(unit):
            qb, a = unit
            rows = slice(qb * BLOCK, (qb + 1) * BLOCK)
            heads = slice(a * HALF, (a + 1) * HALF)
            out = None
            for kb in range(qb + 1):
                keys = slice(kb * BLOCK, (kb + 1) * BLOCK)
                part = mm(v_t[heads, keys], probs[2 * g + a, :, across(kb, qb)])
                out = part if out is None else out + part
                yield
            att_t[g, heads, rows] = (out * inverses[2 * g + a, :, rows]).astype(BF16)

        units = [(qb, a) for qb in range(nblk) for a in range(2)]
        for t in range(len(units) + 2):
            parts = []
            if t < len(units):
                parts.append(scores(units[t], t % 2))
            if 1 <= t <= len(units):
                parts.append(soften(units[t - 1], (t - 1) % 2))
            if t >= 2:
                parts.append(mix(units[t - 2]))
            interleave(parts)
            if t % 2 and t > 1:
                steps_in_loop(g, ATTEND_STEPS, 1 + t // 2)
        return carry

    repeat(pairs, attend, False)

    steps(AFTER_ATTEND)
    for cp in loads[1:]:
        cp.wait()

    blocks = as_matrix(small[0])
    for n in range(4):
        params[n : n + 1, :width] = spread(blocks, n * ROWS, ROWS)
    for j in range(per):
        rows = blocks.shape[0] // per
        params[4:5, j * CHUNK : (j + 1) * CHUNK] = spread(
            blocks[j * rows : (j + 1) * rows], 4 * ROWS, ff * ROWS // width
        )

    sums[...] = jnp.zeros_like(sums)
    gain_one = params[0:1, :width]
    bias_one = params[1:2, :width]
    gain_two = params[2:3, :width]
    bias_two = params[3:4, :width]

    def norm(value):
        mean = jnp.mean(value, axis=1, keepdims=True)
        centred = value - mean
        var = jnp.mean(centred * centred, axis=1, keepdims=True)
        inv = lax.rsqrt(var + EPSILON)
        return centred * inv, inv

    def norm_back(grad, gain, n, inv):
        gn = grad * gain
        m1 = jnp.mean(gn, axis=1, keepdims=True)
        m2 = jnp.mean(gn * n, axis=1, keepdims=True)
        return (gn - m1 - n * m2) * inv

    def add_sum(row, at, value):
        lanes = slice(at, at + value.shape[1])
        sums[row, :, lanes] += jnp.sum(value.reshape(-1, 8, value.shape[1]), axis=0)

    halves = width // BLOCK

    def norm_rows(r0):
        where = [slice(n * slots + r0, n * slots + r0 + NORM_ROWS) for n in range(halves)]
        row = halves * slots + r0 % (BLOCK * 2)
        lanes = slice(r0 // (BLOCK * 2) * PAIR, r0 // (BLOCK * 2) * PAIR + PAIR)
        return where, slice(row, row + NORM_ROWS), lanes

    def keep_norm(r0, value, inv):
        where, rows, lanes = norm_rows(r0)
        for n in range(halves):
            bias[where[n], :] = value[:, n * BLOCK : (n + 1) * BLOCK]
        bias[rows, lanes] = jnp.broadcast_to(inv, (NORM_ROWS, PAIR))

    def kept_norm(r0):
        return jnp.concatenate([bias[rows, :] for rows in norm_rows(r0)[0]], axis=1)

    def kept_factor(r0):
        _, rows, lanes = norm_rows(r0)
        return bias[rows, lanes][:, :1]

    def hold(buf, value):
        for n in range(halves):
            s_scr[buf, n] = value[:, n * BLOCK : (n + 1) * BLOCK]

    def held(buf, r):
        return jnp.concatenate([s_scr[buf, n, r : r + NORM_ROWS, :] for n in range(halves)], axis=1)

    def in_turn(first, second, table):
        for i in range(nblk + 1):
            parts = []
            if i < nblk:
                parts.append(first(i))
            if i:
                parts.append(second(i - 1))
            interleave(parts)
            if table and i:
                steps(table[i - 1][0])

    def attended_rows(i):
        rows = slice(i * BLOCK, (i + 1) * BLOCK)
        at_tile = att_t[:, :, rows].reshape(width, BLOCK).T
        hold(i % 2, mm(at_tile, w_out()))
        yield

    def first_norm_rows(i):
        for r in range(0, BLOCK, NORM_ROWS):
            r0 = i * BLOCK + r
            rows = slice(r0, r0 + NORM_ROWS)
            branch_a = held(i % 2, r)
            n1, inv1 = norm(x_ref[rows, :].astype(F32) + branch_a)
            keep_norm(r0, n1, inv1)
            x_low[rows, :] = (n1 * gain_one + bias_one).astype(BF16)
            y_buf[rows, :] += branch_a
            yield

    in_turn(attended_rows, first_norm_rows, NORM_STEPS)
    steps(AFTER_NORM)

    def up_rows(i, carry):
        rows = pl.ds(aligned(i * BLOCK, BLOCK), BLOCK)
        xl = x_low[rows, :]
        for j in range(per):
            cols = slice(j * CHUNK, (j + 1) * CHUNK)
            u = mm(xl, w_up(j)) + params[4:5, cols]
            u2 = u * u
            t = jnp.tanh(u * (GELU_C + (GELU_C * GELU_K) * u2))
            h = 0.5 + 0.5 * t
            hidden[rows, cols] = (u * h).astype(BF16)
            slope = h + h * (1.0 - h) * (u * (2.0 * GELU_C + (6.0 * GELU_C * GELU_K) * u2))
            du_ref[rows, cols] = slope.astype(BF16)
        steps_in_loop(i, UP_STEPS, 0)
        return carry

    repeat(nblk, up_rows, False)
    steps(AFTER_UP)

    def down_rows(i):
        rows = slice(i * BLOCK, (i + 1) * BLOCK)
        out = None
        for j in range(per):
            part = mm(hidden[rows, j * CHUNK : (j + 1) * CHUNK], w_down(j))
            out = part if out is None else out + part
            yield
        hold(i % 2, out)

    def live_rows(r0):
        return (lax.broadcasted_iota(jnp.int32, (NORM_ROWS, width), 0) + r0) < total

    def second_norm_rows(i):
        for r in range(0, BLOCK, NORM_ROWS):
            r0 = i * BLOCK + r
            rows = slice(r0, r0 + NORM_ROWS)
            branch_f = held(i % 2, r)
            n2, inv2 = norm(kept_norm(r0) * gain_one + bias_one + branch_f)
            live = live_rows(r0)
            gx = jnp.where(live, gx_buf[rows, :].astype(F32), 0.0)
            gy = jnp.where(live, gy_buf[rows, :].astype(F32), 0.0)
            gx_buf[rows, :] = jnp.where(live, n2 * gain_two + bias_two, 0.0).astype(BF16)
            y_buf[rows, :] = jnp.where(live, y_buf[rows, :] + branch_f, 0.0)
            add_sum(3, 0, gx)
            add_sum(2, 0, gx * n2)
            dr2 = norm_back(gx, gain_two, n2, inv2)
            dx_ref[rows, :] = dr2
            df_ref[rows, :] = (dr2 + gy).astype(BF16)
            yield

    in_turn(down_rows, second_norm_rows, None)

    for j in range(per):
        part = mm_tn(hidden[:, j * CHUNK : (j + 1) * CHUNK], df_ref[...]).astype(BF16)
        part = part.reshape(-1, per, ROWS, width)
        for n in range(per):
            grads[pairs + per + n, j] = part[:, n].reshape(GRID[1:] + (ROWS, width))
    steps(AFTER_DOWN)

    def backward_rows(i, carry):
        r0 = aligned(i * BLOCK, BLOCK)
        rows = pl.ds(r0, BLOCK)
        df = df_ref[rows, :]
        dx_mid = dx_ref[rows, :]
        for j in range(per):
            cols = slice(j * CHUNK, (j + 1) * CHUNK)
            du = (mm_nt(df, w_down(j)) * du_ref[rows, cols].astype(F32)).astype(BF16)
            du_ref[rows, cols] = du
            add_sum(4, j * CHUNK, du.astype(F32))
            dx_mid = dx_mid + mm_nt(du, w_up(j))
            if j % 2:
                steps_in_loop(i, BACK_STEPS, j // 2)
        hold(i % 2, dx_mid)
        for r in range(0, BLOCK, NORM_ROWS):
            r1 = r0 + r
            own = slice(r1, r1 + NORM_ROWS)
            grad = held(i % 2, r)
            n1 = kept_norm(r1)
            gy = jnp.where(live_rows(r1), gy_buf[own, :].astype(F32), 0.0)
            add_sum(1, 0, grad)
            add_sum(0, 0, grad * n1)
            dr1 = norm_back(grad, gain_one, n1, kept_factor(r1))
            dx_ref[own, :] = dr1
            gy_buf[own, :] = (dr1 + gy).astype(BF16)
        datt_t[:, :, rows] = mm_nt(w_out(), gy_buf[rows, :]).astype(BF16).reshape(pairs, PAIR, BLOCK)
        steps_in_loop(i, BACK_STEPS, 2)
        return carry

    results = [
        pltpu.make_async_copy(src, dst, out_sem.at[n])
        for n, (src, dst) in enumerate(((gx_buf, xo_hbm), (y_buf, yo_hbm), (dx_ref, dx_hbm)))
    ]
    results[0].start()
    results[1].start()
    repeat(nblk, backward_rows, True)

    def put(p, at, value):
        grads[p, ..., at : at + value.shape[1]] = value.astype(BF16).reshape(
            GRID + (ROWS, value.shape[1])
        )

    for j in range(per):
        put(pairs + j, 0, mm_tn(x_low[...], du_ref[:, j * CHUNK : (j + 1) * CHUNK]))
        steps(UP_SUM_STEPS[j])
    part = mm(att_t[...].reshape(width, slots), gy_buf[...])
    for g in range(pairs):
        put(g, 3 * PAIR, part[:, g * PAIR : (g + 1) * PAIR])

    def gathered(n, lanes, at, r):
        row = jnp.sum(sums[n, :, lanes], axis=0, keepdims=True)
        value = jnp.broadcast_to(row, (row.shape[1] * ROWS // r, width))
        own = lax.broadcasted_iota(jnp.int32, value.shape, 0) // ROWS
        mine = own == lax.broadcasted_iota(jnp.int32, value.shape, 1) // r
        column = lax.broadcasted_iota(jnp.int32, (width, PAIR), 0)
        pick = (lax.broadcasted_iota(jnp.int32, (width, PAIR), 1) == at + column % r).astype(BF16)
        return mm(jnp.where(mine, value, 0.0).astype(BF16), pick)

    rest = [
        gathered(4, slice(j * CHUNK, (j + 1) * CHUNK), 4 * ROWS, ff * ROWS // width)
        for j in range(per)
    ]
    rest = jnp.concatenate(rest, axis=0)
    for n in range(4):
        rest = rest + gathered(n, slice(0, width), n * ROWS, ROWS)
    g_small[0] = rest.astype(BF16).reshape(GRID + (ROWS, PAIR))

    steps(OUT_SUM_STEPS)

    def ds_at(a, kb, qb=None):
        at = (0, nblk, 0, nblk - 2)[kb] * BLOCK
        lanes = slice(at, at + (nblk - kb) * BLOCK)
        if qb is not None:
            lanes = slice(at + (qb - kb) * BLOCK, at + (qb - kb + 1) * BLOCK)
        row = (2 * a + kb // 2) * BLOCK
        return slice(row, row + BLOCK), lanes

    def grads_of(g):
        return pl.ds(aligned(g * 3 * PAIR, PAIR), 3 * PAIR)

    def own_lanes(n, a):
        at = 3 * width + (2 * n + a) * PAIR
        return slice(at, at + PAIR)

    lane = lax.broadcasted_iota(jnp.int32, (slots, PAIR), 1)

    def put_halves(n, value):
        value = value.astype(F32)
        du_ref[:, own_lanes(n, 0)] = jnp.where(lane < HALF, value, 0.0).astype(BF16)
        du_ref[:, own_lanes(n, 1)] = jnp.where(lane < HALF, 0.0, value).astype(BF16)

    turned = slice(slots, 2 * slots)
    key_rows, do_rows = BLOCK, BLOCK + PAIR

    def attend_back(g, carry):
        def put_grad(n, block, value):
            rows = slice(block * BLOCK, (block + 1) * BLOCK)
            lanes = pl.ds(aligned(g * 3 * PAIR + n * PAIR, PAIR), PAIR)
            du_ref[rows, lanes] = value.astype(BF16)

        hidden[key_rows : key_rows + PAIR, turned] = kv_ref[g, :, :PAIR].T
        for a in range(2):
            heads = slice(a * HALF, (a + 1) * HALF)
            scaled = datt_t[g, heads, :].astype(F32) * inverses[2 * g + a]
            dots = jnp.sum(att_t[g, heads, :].astype(F32) * scaled, axis=0, keepdims=True)
            inverses[2 * g + a] = dots
            hidden[do_rows + a * HALF : do_rows + (a + 1) * HALF, turned] = scaled.astype(BF16)
        put_halves(0, hidden[do_rows : do_rows + PAIR, turned].T)
        put_halves(1, q_t[g].T)
        steps_in_loop(g, ATTEND_BACK_STEPS, 0)

        def through_values(unit, buf):
            qb, a = unit
            nk = (qb + 1) * BLOCK
            do = half_rows(hidden[do_rows : do_rows + PAIR, slots + qb * BLOCK : slots + nk], a)
            s_scr[buf, : qb + 1] = mm(kv_ref[g, :nk, PAIR:], do).reshape(qb + 1, BLOCK, BLOCK)
            yield

        def through_softmax(unit, buf):
            qb, a = unit
            dots = inverses[2 * g + a, :, qb * BLOCK : (qb + 1) * BLOCK]
            for r in range(0, (qb + 1) * BLOCK, SPAN):
                inner = slice(r % BLOCK, r % BLOCK + SPAN)
                p = probs[2 * g + a, inner, across(r // BLOCK, qb)].astype(F32)
                rows, lanes = ds_at(a, r // BLOCK, qb)
                ds = p * (s_scr[buf, r // BLOCK, inner] - dots)
                hidden[rows.start + r % BLOCK : rows.start + r % BLOCK + SPAN, lanes] = ds.astype(BF16)
                yield

        def to_queries(unit, kept):
            qb, a = unit
            out = None
            for kb in range(qb + 1):
                keys = slice(slots + kb * BLOCK, slots + (kb + 1) * BLOCK)
                k = hidden[key_rows + a * HALF : key_rows + (a + 1) * HALF, keys]
                part = mm(k, hidden[ds_at(a, kb, qb)])
                out = part if out is None else out + part
                yield
            kept[unit] = out * (HALF**-0.5)
            if a:
                put_grad(0, qb, jnp.concatenate([kept[qb, 0], kept[qb, 1]], axis=0).T)

        def to_values(unit, kept):
            kb, a = unit
            kept[unit] = mm(probs[2 * g + a, :, seen_by(kb)], du_ref[kb * BLOCK :, own_lanes(0, a)])
            yield
            if a:
                put_grad(2, kb, kept[kb, 0] + kept[kb, 1])

        def to_keys(unit, kept):
            kb, a = unit
            kept[unit] = mm(hidden[ds_at(a, kb)], du_ref[kb * BLOCK :, own_lanes(1, a)])
            yield
            if a:
                put_grad(1, kb, kept[kb, 0] + kept[kb, 1])

        kept = {}, {}, {}
        units = [(qb, a) for qb in reversed(range(nblk)) for a in range(2)]
        for t in range(len(units) + 2):
            parts = []
            if t < len(units):
                parts.append(through_values(units[t], t % 2))
                parts.append(to_values(units[t], kept[0]))
            if 1 <= t <= len(units):
                parts.append(through_softmax(units[t - 1], (t - 1) % 2))
            if t >= 2:
                parts.append(to_queries(units[t - 2], kept[1]))
                parts.append(to_keys(units[t - 2], kept[2]))
            interleave(parts)
            if t % 2 and t > 1:
                steps_in_loop(g, ATTEND_BACK_STEPS, t // 2)
        put(g, 0, mm(x_t[...], du_ref[:, grads_of(g)]))
        steps_in_loop(g, ATTEND_BACK_STEPS, 1 + nblk)
        return carry

    repeat(pairs, attend_back, True)

    for qb in range(nblk):
        rows = slice(qb * BLOCK, (qb + 1) * BLOCK)
        total_dx = dx_ref[rows, :]
        for g in range(pairs):
            grad = du_ref[rows, g * 3 * PAIR : (g + 1) * 3 * PAIR]
            total_dx = total_dx + mm_nt(grad, w_qkv(g))
        dx_ref[rows, :] = total_dx
        steps(INPUT_STEPS[qb])
    results[2].start()
    steps(LAST_STEPS)
    for cp in results:
        cp.wait()
    if linked:
        gather_small.step(5, 0)
        scatter_small.step(5, 0)
        for p in range(PIECES):
            gather.step(5, p)
            scatter.step(5, p)


def layer(linked, x_in, y_in, lengths, grad_x, grad_y, *rest):
    slots, width = x_in.shape
    ff = 4 * width
    nblk = slots // BLOCK
    pairs = H // 2
    causal = BLOCK * nblk * (nblk + 1) // 2
    vmem = pl.BlockSpec(memory_space=pltpu.VMEM)
    any_ = pl.BlockSpec(memory_space=pl.ANY)
    smem = pl.BlockSpec(memory_space=pltpu.SMEM)
    streams = tuple(jax.ShapeDtypeStruct((slots, width), dtype) for dtype in (BF16, F32, F32))
    wide = (PIECES,) + GRID + (ROWS, CHUNK)
    narrow = (1,) + GRID + (ROWS, PAIR)
    links = []
    if linked:
        outs = [
            jax.ShapeDtypeStruct((PIECES, ROWS, CHUNK), F32),
            jax.ShapeDtypeStruct((ROWS, PAIR), F32),
        ]
        links += [pltpu.VMEM(wide, BF16), pltpu.VMEM(wide, BF16)]
        links += [pltpu.VMEM(narrow, BF16), pltpu.VMEM(narrow, BF16)]
        for n, _, _, _, _, r, lanes in (wide, narrow):
            links += [
                pltpu.VMEM((n, 4, 2, 2, r, lanes), BF16),
                pltpu.VMEM((n, 2, 2, 2, r, lanes), BF16),
                pltpu.VMEM((n, 2, 2, r, lanes), BF16),
                pltpu.VMEM((n, 3, r, lanes), BF16),
                pltpu.VMEM((3, 4, r, lanes), BF16),
            ]
        for n in (PIECES, 1, PIECES, 1):
            links += [pltpu.SemaphoreType.DMA((n, Z + 4)), pltpu.SemaphoreType.DMA((n, Z + 4))]
        params = pltpu.CompilerParams(
            vmem_limit_bytes=VMEM_LIMIT, collective_id=0, has_side_effects=True
        )
    else:
        outs = [jax.ShapeDtypeStruct(wide, BF16), jax.ShapeDtypeStruct(narrow, BF16)]
        params = pltpu.CompilerParams(vmem_limit_bytes=VMEM_LIMIT)
    return pl.pallas_call(
        functools.partial(layer_kernel, linked),
        out_shape=streams + tuple(outs),
        in_specs=[smem] + [any_] * 4 + [vmem] * len(rest),
        out_specs=(any_,) * 3 + (vmem,) * len(outs),
        scratch_shapes=links
        + [
            pltpu.VMEM((slots, width), BF16),
            pltpu.VMEM((slots, width), BF16),
            pltpu.VMEM((slots, width), F32),
            pltpu.VMEM((slots, width), F32),
            pltpu.VMEM((slots, width), BF16),
            pltpu.VMEM((8, ff), F32),
            pltpu.VMEM((5, 8, ff), F32),
            pltpu.VMEM((pairs, slots, 2 * PAIR), BF16),
            pltpu.VMEM((pairs, PAIR, slots), BF16),
            pltpu.VMEM((pairs, PAIR, slots), BF16),
            pltpu.VMEM((H, 1, slots), F32),
            pltpu.VMEM((pairs, PAIR, slots), BF16),
            pltpu.VMEM((H, BLOCK, causal), BF16),
            pltpu.VMEM((causal, BLOCK), F32),
            pltpu.VMEM((slots, ff), BF16),
            pltpu.VMEM((slots, ff), BF16),
            pltpu.VMEM((slots, width), BF16),
            pltpu.VMEM((slots, width), BF16),
            pltpu.VMEM((width, slots), BF16),
            pltpu.VMEM((2, nblk, BLOCK, BLOCK), F32),
            pltpu.SemaphoreType.DMA((4,)),
            pltpu.SemaphoreType.DMA((3,)),
        ],
        compiler_params=params,
        name="layer",
    )(lengths, x_in, y_in, grad_x, grad_y, *rest)


def deliver_kernel(x_out, y_out, d_x, shares, small, *refs):
    streams, (d_qkv, d_out, d_up, d_down), vectors = refs[:3], refs[3:7], refs[7:12]
    buffers, (load_sem, store_sem) = refs[12:15], refs[15:]
    loads, stores = [], []
    for n, (src, buf, dst) in enumerate(zip((x_out, y_out, d_x), buffers, streams)):
        loads.append(pltpu.make_async_copy(src, buf, load_sem.at[n]))
        stores.append(pltpu.make_async_copy(buf, dst, store_sem.at[n]))
    for cp in loads:
        cp.start()
    pairs, width = H // 2, d_out.shape[1]
    for g in range(pairs):
        for n in range(3):
            lanes = slice(n * width + g * PAIR, n * width + (g + 1) * PAIR)
            d_qkv[:, lanes] = shares[g, :, n * PAIR : (n + 1) * PAIR]
        d_out[:, g * PAIR : (g + 1) * PAIR] = shares[g, :, 3 * PAIR :]
    per = d_up.shape[1] // CHUNK
    for j in range(per):
        d_up[:, j * CHUNK : (j + 1) * CHUNK] = shares[pairs + j]
        d_down[j * ROWS : (j + 1) * ROWS, :] = shares[pairs + per + j]
    at = 0
    for ref in vectors:
        ref[...] = small[0, at : at + ref.shape[0]]
        at += ref.shape[0]
    for load, store in zip(loads, stores):
        load.wait()
        store.start()
    for store in stores:
        store.wait()


def deliver(streams, shares, small, shapes):
    vmem = pl.BlockSpec(memory_space=pltpu.VMEM)
    any_ = pl.BlockSpec(memory_space=pl.ANY)
    outs = [jax.ShapeDtypeStruct(s.shape, s.dtype) for s in streams]
    outs += [jax.ShapeDtypeStruct(shape, F32) for shape in shapes]
    return pl.pallas_call(
        deliver_kernel,
        out_shape=outs,
        in_specs=[any_] * 3 + [vmem] * 2,
        out_specs=[any_] * 3 + [vmem] * 9,
        scratch_shapes=[pltpu.VMEM(s.shape, s.dtype) for s in streams]
        + [pltpu.SemaphoreType.DMA((3,)), pltpu.SemaphoreType.DMA((3,))],
        compiler_params=pltpu.CompilerParams(vmem_limit_bytes=VMEM_LIMIT),
        name="deliver",
    )(*streams, shares, small)


BOTH = ("dp", "fsdp")


def on_device(
    linked,
    x_in,
    y_in,
    lengths,
    w_qkv,
    w_out,
    gain_one,
    bias_one,
    w_up,
    b_up,
    w_down,
    gain_two,
    bias_two,
    grad_x,
    grad_y,
):
    streams = (x_in, y_in, lengths, grad_x, grad_y)
    width = x_in.shape[1]
    if linked:
        ends = (gain_one, bias_one, gain_two, bias_two, b_up)
        *out_streams, shares, small = layer(True, *streams, w_qkv, w_out, w_up, w_down, *ends)
        shapes = [w.shape for w in (w_qkv, w_out, w_up, w_down) + ends]
        x_out, y_out, d_x, d_qkv, d_out, d_up, d_down, *vectors = deliver(
            out_streams, shares, small, shapes
        )
    else:
        blocks = GRID[0] * GRID[1] * GRID[2] * GRID[3]
        pairs = H // 2

        def whole(w):
            return lax.all_gather(w, BOTH, axis=0, tiled=True)

        def cut(w):
            return w.reshape(GRID + (ROWS, CHUNK))

        qkv, out, up, down = (whole(w) for w in (w_qkv, w_out, w_up, w_down))
        pieces = []
        for g in range(pairs):
            lane = [slice(n * width + g * PAIR, n * width + (g + 1) * PAIR) for n in range(3)]
            pieces.append(cut(jnp.concatenate([qkv[:, s] for s in lane] + [out[:, lane[0]]], 1)))
        per = up.shape[1] // CHUNK
        pieces += [cut(up[:, j * CHUNK : (j + 1) * CHUNK]) for j in range(per)]
        down = down.reshape(blocks, per, ROWS, width)
        pieces += [cut(down[:, j].reshape(-1, width)) for j in range(per)]
        vectors = [whole(v) for v in (gain_one, bias_one, gain_two, bias_two, b_up)]
        small = jnp.concatenate([v.reshape(blocks, -1) for v in vectors], axis=1)
        small = jnp.broadcast_to(small[:, None], (blocks, ROWS, small.shape[1]))
        x_out, y_out, d_x, grads, d_small = layer(
            False, *streams, jnp.stack(pieces), small.reshape((1,) + GRID + (ROWS, -1))
        )

        def share(w):
            return lax.psum_scatter(w, BOTH, scatter_dimension=0, tiled=True)

        grads = grads.astype(F32).reshape(PIECES, -1, CHUNK)
        d_qkv = grads[:pairs, :, : 3 * PAIR].reshape(pairs, width, 3, PAIR)
        d_qkv = share(d_qkv.transpose(1, 2, 0, 3).reshape(width, 3 * width))
        d_out = share(grads[:pairs, :, 3 * PAIR :].transpose(1, 0, 2).reshape(width, width))
        d_up = share(grads[pairs : pairs + per].transpose(1, 0, 2).reshape(width, -1))
        d_down = grads[pairs + per :].reshape(per, blocks, ROWS, width).transpose(1, 0, 2, 3)
        d_down = share(d_down.reshape(-1, width))
        rows = d_small.astype(F32).reshape(blocks, ROWS, -1)[:, 0]
        vectors = [share(rows[:, n * ROWS : (n + 1) * ROWS].reshape(-1)) for n in range(4)]
        vectors.append(share(rows[:, 4 * ROWS :].reshape(-1)))
    return (
        x_out,
        y_out,
        d_x,
        d_qkv,
        d_out,
        vectors[0],
        vectors[1],
        d_up,
        vectors[4],
        d_down,
        vectors[2],
        vectors[3],
    )


def solution(mesh):
    matrix, vector = P(BOTH, None), P(BOTH)
    linked = mesh.shape["dp"] == Z and mesh.shape["fsdp"] == GRID[1] * GRID[2] * GRID[3]
    return jax.shard_map(
        functools.partial(on_device, linked),
        mesh=mesh,
        in_specs=(matrix,) * 5
        + (vector, vector, matrix, vector, matrix, vector, vector, matrix, matrix),
        out_specs=(matrix,) * 5
        + (vector, vector, matrix, vector, matrix, vector, vector),
        check_vma=False,
    )
```
